1024 devices in a mesh: ctx: 64 (over y, x), head: 16 (over z, core).
Axes of the slice: x: 8, y: 8, z: 8, core: 2. Of those that a mesh axis runs over, the one named last changes fastest.
Arguments:
- inputs: bfloat16 [32768, 4096], P('ctx', 'head'), may hold values from -6 to 6
- write_map: bfloat16 [32768, 128], P('ctx'), may hold values from -2 to 2
- read_map: bfloat16 [32768, 128], P('ctx'), may hold values from -2 to 2
- step_scale: float32 [64, 32768], P('head', 'ctx'), may hold values from 0 to 1, as said below
- log_decay: float32 [64, 32768], P('head', 'ctx'), may hold values from -1 to 0, as said below
- lengths: int32 [4], replicated, may hold values from 1 to 16384, 32768 in all
- out_grad: bfloat16 [32768, 4096], P('ctx', 'head'), may hold values from -1.5 to 1.5
Outputs:
- outputs: bfloat16 [32768, 4096], P('ctx', 'head')
- input_grad: bfloat16 [32768, 4096], P('ctx', 'head')
- write_grad: float32 [32768, 128], P(('ctx', 'head'))
- read_grad: float32 [32768, 128], P(('ctx', 'head'))
- step_grad: float32 [64, 32768], P('head', 'ctx')
- decay_grad: float32 [64, 32768], P('head', 'ctx')
The draws below stay inside these ranges and needn't reach their ends.
Inputs may be any that keep to these rules, and one draw needn't show every extreme that they name: The lengths add up to 32768; the longest is exactly 16384. `log_decay`: zero or negative. `step_scale`: Positive.
All inputs are finite; a program needn't handle non-finite values.
Results may differ from the reference program's by a relative error of at most 0.0019.
Values sent between devices are 32-bit elements; how exact they have to be, the bound alone decides.
No kernel may reach another device: no remote copies, remote signals or barrier semaphores. Data moves between devices by JAX's collectives and lax.ppermute only.
A program may use at most 64 MiB of HBM per device.

```python
import math
import jax
import jax.numpy as jnp
import numpy as np
from jax import lax

P_SIZE = 64
NS = 128
TOK_DEV = 512
RECS = 4
HEADS = 64
TOKEN_STEPS = 32768
LONGEST = 16384


surge_count = 8


def head_rates(key, fast_share):
    first_key, second_key, third_key = jax.random.split(key, 3)
    slow_rate = jnp.exp(jax.random.uniform(first_key, (HEADS,), jnp.float32, math.log(0.3), math.log(2.3))) / TOKEN_STEPS
    fast_rate = jnp.exp(jax.random.uniform(second_key, (HEADS,), jnp.float32, math.log(0.02), math.log(1.0 / 30.0)))
    picked = jax.random.uniform(third_key, (HEADS,), jnp.float32) < fast_share
    return jnp.where(picked, fast_rate, slow_rate)


def draw_log_decay(key, part):
    share = 0.5
    rates = head_rates(key, share)
    key = jax.random.fold_in(key, 3)
    rough_key, location_key, loss_key = jax.random.split(key, 3)
    rough = jnp.exp(jax.random.uniform(rough_key, (HEADS, TOKEN_STEPS), jnp.float32, math.log(0.5), math.log(2.0)))
    location_points = jax.random.randint(location_key, (surge_count,), 0, TOKEN_STEPS)
    struck = jnp.any(jnp.arange(TOKEN_STEPS)[:, None] == location_points[None, :], axis=1)
    losses = jax.random.uniform(loss_key, (HEADS, TOKEN_STEPS), jnp.float32, 0.2, 0.5)
    return jnp.where(struck[None, :], jnp.log(1.0 - losses), -rates[:, None] * rough)


def draw_step_scale(key, part):
    share = 0.5
    rates = head_rates(key, share)
    key = jax.random.fold_in(key, 5)
    rough = jnp.exp(jax.random.uniform(key, (HEADS, TOKEN_STEPS), jnp.float32, math.log(0.5), math.log(2.0)))
    return jnp.sqrt(2.0 * rates)[:, None] * rough


def block_scale(key, dims, cuts, smallest, high):
    level, own = 1.0, jax.random.fold_in(key, 6)
    for position, blocks in cuts:
        heights = jnp.exp(jax.random.uniform(jax.random.fold_in(own, position), (blocks,), jnp.float32, smallest / len(cuts), high / len(cuts)))
        level = level * jnp.repeat(heights, dims[position] // blocks).reshape([-1 if axis == position else 1 for axis in range(len(dims))])
    return level


def split_up(amount, total, most, lean):
    loads = [(1 << 20) // math.isqrt(standing ** lean) + 1 for standing in range(2, amount + 1)]
    surplus, given = total - most - (amount - 1), [1] * (amount - 1)
    while surplus > 0:
        movable = [i for i in range(amount - 1) if given[i] < most]
        pool, budget = sum([loads[i] for i in movable]), surplus
        for i in movable:
            extra = min(most - given[i], max(1, budget * loads[i] // pool), surplus)
            given[i] = given[i] + extra
            surplus = surplus - extra
    return np.array([most] + given)


def ragged_sizes(rng, amount, total, bound, lean):
    if amount == 2:
        one = jax.random.randint(rng, (), max(1, total - bound), min(bound, total - 1) + 1)
        return jnp.stack([one, total - one])
    sizes = jnp.asarray(split_up(amount, total, bound, lean), jnp.int32)
    pairs = (amount - 1) // 2
    source_of, receiver = sizes[1:1 + 2 * pairs:2], sizes[2:2 + 2 * pairs:2]
    margin = jnp.minimum(source_of - 1, bound - receiver)
    shifted = jax.random.randint(jax.random.fold_in(rng, 1), (pairs,), 0, 1 << 20) % (margin + 1)
    sizes = sizes.at[1:1 + 2 * pairs:2].set(source_of - shifted).at[2:2 + 2 * pairs:2].set(receiver + shifted)
    return sizes[jax.random.permutation(jax.random.fold_in(rng, 2), amount)]


def gaussian(key, shape, deviation, bound, cuts=(), kind=jnp.bfloat16):
    loudness = block_scale(key, shape, cuts, -0.22, 0.18) if cuts else 1.0
    entries = jax.random.normal(key, shape, jnp.float32) * deviation * loudness
    return jnp.minimum(jnp.maximum(entries, -bound), bound).astype(kind)


def setup_inputs(seed: int = 0) -> dict:
    arg_keys = jax.random.split(jax.random.key(seed), 8)
    return {
        "inputs": gaussian(arg_keys[0], (TOKEN_STEPS, HEADS * P_SIZE), 1.0, 6.0, ((0, 64), (1, 16))),
        "write_map": gaussian(arg_keys[1], (TOKEN_STEPS, NS), 0.3, 2.0, ((0, 64),)),
        "read_map": gaussian(arg_keys[2], (TOKEN_STEPS, NS), 0.3, 2.0, ((0, 64),)),
        "step_scale": draw_step_scale(jax.random.fold_in(arg_keys[7], 71), 0),
        "log_decay": draw_log_decay(jax.random.fold_in(arg_keys[7], 71), 0),
        "lengths": ragged_sizes(arg_keys[5], RECS, TOKEN_STEPS, LONGEST, 2).astype(jnp.int32),
        "out_grad": gaussian(arg_keys[6], (TOKEN_STEPS, HEADS * P_SIZE), 0.25, 1.5, ((0, 64), (1, 16))),
    }


def reference(inputs, write_map, read_map, step_scale, log_decay, lengths, out_grad):
    block_rows = min(TOK_DEV, 256)
    block_count = TOKEN_STEPS // block_rows
    highest = lax.Precision.HIGHEST
    record_ends = jnp.cumsum(lengths).astype(jnp.int32)
    record_starts = (record_ends - lengths).astype(jnp.int32)
    positions = jnp.arange(TOKEN_STEPS, dtype=jnp.int32)
    record_id = lax.optimization_barrier(jnp.sum((record_starts[None, :] <= positions[:, None]).astype(jnp.int32), axis=1)).astype(jnp.int32)
    record_id_blocks = record_id.reshape(block_count, block_rows)
    shifted_ids = jnp.concatenate([jnp.zeros((1,), jnp.int32), record_id[:-1]]).astype(jnp.int32)
    id_before = shifted_ids.reshape(block_count, block_rows)[:, 0]
    local_index = jnp.arange(block_rows, dtype=jnp.int32)

    def one_block(carried_state, pieces):
        x_block, write_block, read_block, step_block, block_decay_factor, id_block, id_prev = pieces
        cumulative = jnp.cumsum(block_decay_factor, axis=1)
        inside = (local_index[None, :] <= local_index[:, None]) & (id_block[:, None] == id_block[None, :])
        gap_log = jnp.where(inside[None], cumulative[:, :, None] - cumulative[:, None, :], 0.0)
        decays = jnp.exp(gap_log) * inside[None].astype(jnp.float32)
        scores = jnp.dot(read_block, write_block.T, precision=highest)
        weights = scores[None] * decays * step_block[:, None, :]
        local_out = jnp.einsum('hts,shp->thp', weights, x_block, precision=highest)
        enter = jnp.where(id_block[None, :] == id_prev, jnp.exp(cumulative), 0.0)
        carried_out = jnp.einsum('tn,hpn->thp', read_block, carried_state, precision=highest)
        result_y = local_out + enter.T[:, :, None] * carried_out
        leave = jnp.where(id_block[None, :] == id_block[-1], jnp.exp(cumulative[:, -1:] - cumulative), 0.0)
        fresh = jnp.einsum('hs,shp,sn->hpn', leave * step_block, x_block, write_block, precision=highest)
        keep_factor = jnp.where(id_block[-1] == id_prev, jnp.exp(cumulative[:, -1]), 0.0)
        return (keep_factor[:, None, None] * carried_state + fresh, result_y)

    def forward(x_full, write_full, read_full, step_full, decay_full):
        pieces = (x_full.reshape(block_count, block_rows, HEADS, P_SIZE), write_full.reshape(block_count, block_rows, NS), read_full.reshape(block_count, block_rows, NS), step_full.reshape(HEADS, block_count, block_rows).transpose(1, 0, 2), decay_full.reshape(HEADS, block_count, block_rows).transpose(1, 0, 2), record_id_blocks, id_before)
        start_state = jnp.zeros((HEADS, P_SIZE, NS), jnp.float32)
        final_state, result_y = lax.scan(jax.checkpoint(one_block), start_state, pieces)
        return result_y.reshape(TOKEN_STEPS, HEADS, P_SIZE)
    x_full = inputs.astype(jnp.float32).reshape(TOKEN_STEPS, HEADS, P_SIZE)
    result_y, pull_back = jax.vjp(forward, x_full, write_map.astype(jnp.float32), read_map.astype(jnp.float32), step_scale, log_decay)
    grads = pull_back(out_grad.astype(jnp.float32).reshape(TOKEN_STEPS, HEADS, P_SIZE))
    outputs = result_y.reshape(TOKEN_STEPS, HEADS * P_SIZE).astype(jnp.bfloat16)
    input_grad = grads[0].reshape(TOKEN_STEPS, HEADS * P_SIZE).astype(jnp.bfloat16)
    return (outputs, input_grad, grads[1], grads[2], step_scale * grads[3], log_decay * grads[4])
```

```python
import jax
import jax.numpy as jnp
from jax import lax
from jax.experimental import pallas as pl
from jax.experimental.pallas import tpu as pltpu
from jax.sharding import PartitionSpec as P

F32 = jnp.float32
BF16 = jnp.bfloat16
CHUNK = 128
NEG = -1e30


def split(v):
    hi = v.astype(BF16)
    return hi, (v - hi.astype(F32)).astype(BF16)


def mm(a, b, ca, cb):
    return lax.dot_general(a, b, (((ca,), (cb,)), ((), ())), preferred_element_type=F32)


def mm_exact(a, b, ca, cb):
    return lax.dot_general(
        a, b, (((ca,), (cb,)), ((), ())),
        precision=lax.Precision.HIGHEST, preferred_element_type=F32,
    )


def iota(shape, dim):
    return lax.broadcasted_iota(jnp.int32, shape, dim)


def records_at(len_ref, pos):
    start = jnp.int32(0)
    total = (pos >= start).astype(jnp.int32)
    for k in range(len_ref.shape[0] - 1):
        start = start + len_ref[k]
        total = total + (pos >= start).astype(jnp.int32)
    return total


def scalar_record(len_ref, pos):
    start = jnp.int32(0)
    total = jnp.where(pos >= start, 1, 0)
    for k in range(len_ref.shape[0] - 1):
        start = start + len_ref[k]
        total = total + jnp.where(pos >= start, 1, 0)
    return total


def running_sums(rows):
    heads, steps = rows.shape
    chunks = steps // CHUNK
    stacked = jnp.concatenate([rows[:, q * CHUNK:(q + 1) * CHUNK] for q in range(chunks)], axis=0)
    tri = (iota((CHUNK, CHUNK), 0) <= iota((CHUNK, CHUNK), 1)).astype(F32)
    sums = mm_exact(stacked, tri, 1, 0)
    return [sums[q * heads:(q + 1) * heads, :] for q in range(chunks)]


def block_rows(len_ref, offset, ld, dt):
    heads, steps = ld.shape
    parts = running_sums(ld)
    total = jnp.zeros((heads, 1), F32)
    cums = []
    for part in parts:
        cums.append(part + total)
        total = total + part[:, CHUNK - 1:CHUNK]
    cum = jnp.concatenate(cums, axis=1)
    rec = records_at(len_ref, offset + iota((1, steps), 1))
    last = scalar_record(len_ref, offset + steps - 1)
    prev = scalar_record(len_ref, offset - 1)
    enter = jnp.exp(jnp.where(rec == prev, cum, NEG))
    leave = jnp.exp(jnp.where(rec == last, total - cum, NEG))
    keep = jnp.exp(jnp.where(last == prev, total, NEG))
    return enter, leave, keep


def lanes_of(cols, first, heads):
    rows = cols.shape[0]
    low = iota((rows, 128), 1) < 64
    out = []
    for h in range(0, heads, 2):
        a = cols[:, first + h:first + h + 1]
        b = cols[:, first + h + 1:first + h + 2]
        out.append(jnp.where(low, a, b))
    return jnp.concatenate(out, axis=1)


def state_terms(len_ref, off_ref, ld_ref, dt_ref, w_ref, r_ref, x_ref, g_ref, pay_ref):
    heads, steps = ld_ref.shape
    offset = off_ref[0]
    dt = dt_ref[...]
    enter, leave, keep = block_rows(len_ref, offset, ld_ref[...], dt)
    stack = jnp.concatenate([leave * dt, enter], axis=0)
    xs, gs = [], []
    for q in range(steps // CHUNK):
        rows = pl.ds(q * CHUNK, CHUNK)
        cols = jnp.transpose(stack[:, q * CHUNK:(q + 1) * CHUNK])
        xs.append(x_ref[rows, :].astype(F32) * lanes_of(cols, 0, heads))
        gs.append(g_ref[rows, :].astype(F32) * lanes_of(cols, heads, heads))
    x_hi, x_lo = split(jnp.concatenate(xs, axis=0))
    g_hi, g_lo = split(jnp.concatenate(gs, axis=0))
    w = w_ref[...]
    r = r_ref[...]
    fresh = mm(w, x_hi, 0, 0) + mm(w, x_lo, 0, 0)
    back = mm(r, g_hi, 0, 0) + mm(r, g_lo, 0, 0)
    low = iota((32, 128), 1) < 64
    for half in range(2):
        lanes = slice(128 * half, 128 * half + 128)
        for i in range(4):
            rows = slice(32 * i, 32 * i + 32)
            pay_ref[pl.ds(512 * half + i, 32, stride=16), :] = fresh[rows, lanes]
            pay_ref[pl.ds(512 * half + 4 + i, 32, stride=16), :] = back[rows, lanes]
        pair = jnp.where(low, keep[2 * half:2 * half + 1, :], keep[2 * half + 1:2 * half + 2, :])
        pay_ref[pl.ds(512 * half + 8, 32, stride=16), :] = pair


def scan_blocks(in_ref, out_ref):
    blocks = in_ref.shape[0] // 16
    forward = iota((8, 128), 0) < 4
    carry = jnp.zeros((8, 128), F32)
    held = []
    for j in range(blocks):
        held.append(carry)
        carry = carry * in_ref[16 * j + 8:16 * j + 9, :] + in_ref[16 * j:16 * j + 8, :]
    carry = jnp.zeros((8, 128), F32)
    for j in range(blocks - 1, -1, -1):
        out_ref[8 * j:8 * j + 8, :] = jnp.where(forward, held[j], carry)
        carry = carry * in_ref[16 * j + 8:16 * j + 9, :] + in_ref[16 * j:16 * j + 8, :]


def read_states(st_ref):
    both = []
    for kind in range(2):
        halves = []
        for half in range(2):
            halves.append(jnp.concatenate(
                [st_ref[pl.ds(256 * half + 4 * kind + i, 32, stride=8), :] for i in range(4)],
                axis=0))
        both.append(jnp.concatenate(halves, axis=1))
    return both


def local_part(len_ref, off_ref, ld_ref, dt_ref, w_ref, r_ref, x_ref, g_ref,
               y_ref, p_ref, wl_ref, rl_ref, xh_ref, xl_ref, gh_ref, gl_ref):
    heads, steps = ld_ref.shape
    chunks = steps // CHUNK
    offset = off_ref[0]
    ld = ld_ref[...]
    dt_all = dt_ref[...]
    enter_b, leave_b, _ = block_rows(len_ref, offset, ld, dt_all)
    parts = running_sums(ld)
    low = iota((CHUNK, 128), 1) < 64
    causal = iota((CHUNK, CHUNK), 1) <= iota((CHUNK, CHUNK), 0)
    saved = []
    for q in range(chunks):
        rows = pl.ds(q * CHUNK, CHUNK)
        span = slice(q * CHUNK, (q + 1) * CHUNK)
        first = offset + q * CHUNK
        cum = parts[q]
        total = cum[:, CHUNK - 1:CHUNK]
        dt = dt_all[:, span]
        rec_row = records_at(len_ref, first + iota((1, CHUNK), 1))
        rec_col = records_at(len_ref, first + iota((CHUNK, 1), 0))
        last = scalar_record(len_ref, first + CHUNK - 1)
        prev = scalar_record(len_ref, first - 1)
        enter = jnp.exp(jnp.where(rec_row == prev, cum, NEG))
        leave = jnp.exp(jnp.where(rec_row == last, total - cum, NEG))
        keep = jnp.exp(jnp.where(last == prev, total, NEG))
        stack = jnp.concatenate(
            [cum, enter, leave, leave * dt, leave_b[:, span] * dt, enter_b[:, span]], axis=0)
        cols = jnp.transpose(stack)
        x = x_ref[rows, :]
        g = g_ref[rows, :]
        xf = x.astype(F32)
        gf = g.astype(F32)
        xb_hi, xb_lo = split(xf * lanes_of(cols, 4 * heads, heads))
        gb_hi, gb_lo = split(gf * lanes_of(cols, 5 * heads, heads))
        xh_ref[rows, :] = xb_hi
        xl_ref[rows, :] = xb_lo
        gh_ref[rows, :] = gb_hi
        gl_ref[rows, :] = gb_lo
        enter_lanes = lanes_of(cols, heads, heads)
        leave_lanes = lanes_of(cols, 2 * heads, heads)
        xc = split(xf * lanes_of(cols, 3 * heads, heads))
        gc = split(gf * enter_lanes)
        w = w_ref[rows, :]
        r = r_ref[rows, :]
        fresh = mm(w, xc[0], 0, 0) + mm(w, xc[1], 0, 0)
        back = mm(r, gc[0], 0, 0) + mm(r, gc[1], 0, 0)
        keep_row = jnp.concatenate([
            jnp.where(iota((1, 128), 1) < 64, keep[h:h + 1, :], keep[h + 1:h + 2, :])
            for h in range(0, heads, 2)], axis=1)
        inside = causal & (rec_row == rec_col)
        scores = mm(r, w, 1, 1)
        total_e = jnp.zeros((CHUNK, CHUNK), F32)
        y_parts, p_parts = [], []
        for h in range(heads):
            pair = slice(128 * (h // 2), 128 * (h // 2) + 128)
            x_pair = x[:, pair]
            g_pair = g[:, pair]
            mine = low if h % 2 == 0 else ~low
            decays = jnp.exp(jnp.where(inside, cols[:, h:h + 1] - cum[h:h + 1, :], NEG))
            weighted = scores * decays
            dt_row = dt[h:h + 1, :]
            a_hi, a_lo = split(weighted * dt_row)
            y_parts.append(mm(a_hi, x_pair, 1, 0) + mm(a_lo, x_pair, 1, 0))
            b_hi, b_lo = split(weighted)
            p_parts.append(mm(b_hi, g_pair, 0, 0) + mm(b_lo, g_pair, 0, 0))
            g_mine = jnp.where(mine, gf[:, pair], 0.0).astype(BF16)
            total_e = total_e + decays * dt_row * mm(g_mine, x_pair, 1, 1)
        y = jnp.concatenate([jnp.where(low, y_parts[h], y_parts[h + 1]) for h in range(0, heads, 2)], axis=1)
        p = jnp.concatenate([jnp.where(low, p_parts[h], p_parts[h + 1]) for h in range(0, heads, 2)], axis=1)
        e_hi, e_lo = split(total_e)
        wl = mm(e_hi, r, 0, 0) + mm(e_lo, r, 0, 0)
        rl = mm(e_hi, w, 1, 0) + mm(e_lo, w, 1, 0)
        saved.append((rows, y, p, wl, rl, xc, gc, w, r, fresh, back, keep_row, enter_lanes, leave_lanes))
    state = None
    for q in range(chunks):
        rows, y, p, wl, rl, xc, gc, w, r, fresh, back, keep_row, enter_lanes, leave_lanes = saved[q]
        if state is not None:
            s_hi, s_lo = split(state)
            y = y + enter_lanes * (mm(r, s_hi, 1, 0) + mm(r, s_lo, 1, 0))
            rl = rl + (mm(gc[0], s_hi, 1, 1) + mm(gc[0], s_lo, 1, 1) + mm(gc[1], s_hi, 1, 1))
            state = state * keep_row + fresh
        else:
            state = fresh
        y_ref[rows, :] = y
        rl_ref[rows, :] = rl
    future = None
    for q in range(chunks - 1, -1, -1):
        rows, y, p, wl, rl, xc, gc, w, r, fresh, back, keep_row, enter_lanes, leave_lanes = saved[q]
        if future is not None:
            f_hi, f_lo = split(future)
            p = p + leave_lanes * (mm(w, f_hi, 1, 0) + mm(w, f_lo, 1, 0))
            wl = wl + (mm(xc[0], f_hi, 1, 1) + mm(xc[0], f_lo, 1, 1) + mm(xc[1], f_hi, 1, 1))
            future = future * keep_row + back
        else:
            future = back
        p_ref[rows, :] = p
        wl_ref[rows, :] = wl


def shared_grads(st_ref, wl_ref, rl_ref, xh_ref, xl_ref, gh_ref, gl_ref, out_ref):
    steps = wl_ref.shape[0]
    incoming, future = read_states(st_ref)
    s_hi, s_lo = split(incoming)
    f_hi, f_lo = split(future)
    xh = xh_ref[...]
    gh = gh_ref[...]
    w = wl_ref[...] + mm(xh, f_hi, 1, 1) + mm(xh, f_lo, 1, 1) + mm(xl_ref[...], f_hi, 1, 1)
    r = rl_ref[...] + mm(gh, s_hi, 1, 1) + mm(gh, s_lo, 1, 1) + mm(gl_ref[...], s_hi, 1, 1)
    share = steps // out_ref.shape[0]
    out_ref[:, 0:share, :] = w.reshape(out_ref.shape[0], share, w.shape[1])
    out_ref[:, share:2 * share, :] = r.reshape(out_ref.shape[0], share, r.shape[1])


def finish(len_ref, off_ref, ld_ref, dt_ref, w_ref, r_ref, x_ref, g_ref, y_ref, p_ref, st_ref,
           out_ref, xg_ref, sg_ref, dg_ref):
    heads, steps = ld_ref.shape
    chunks = steps // CHUNK
    offset = off_ref[0]
    ld = ld_ref[...]
    dt = dt_ref[...]
    enter, leave, keep = block_rows(len_ref, offset, ld, dt)
    incoming, future = read_states(st_ref)
    s_hi, s_lo = split(incoming)
    f_hi, f_lo = split(future)
    width = x_ref.shape[1]
    pick = (iota((8, width), 1) // 64 == iota((8, width), 0)).astype(F32)
    stack = jnp.concatenate([enter, leave, dt, dt], axis=0)
    p_rows, ql_rows, qs_rows = [], [], []
    for q in range(chunks):
        rows = pl.ds(q * CHUNK, CHUNK)
        cols = jnp.transpose(stack[:, q * CHUNK:(q + 1) * CHUNK])
        r = r_ref[rows, :]
        w = w_ref[rows, :]
        y = y_ref[rows, :] + lanes_of(cols, 0, heads) * (mm(r, s_hi, 1, 0) + mm(r, s_lo, 1, 0))
        near = p_ref[rows, :]
        far = lanes_of(cols, heads, heads) * (mm(w, f_hi, 1, 0) + mm(w, f_lo, 1, 0))
        out_ref[rows, :] = y.astype(BF16)
        xg_ref[rows, :] = (lanes_of(cols, 2 * heads, heads) * (near + far)).astype(BF16)
        xf = x_ref[rows, :].astype(F32)
        p_rows.append(mm_exact(pick, g_ref[rows, :].astype(F32) * y, 1, 1)[0:heads, :])
        ql_rows.append(mm_exact(pick, xf * near, 1, 1)[0:heads, :])
        qs_rows.append(mm_exact(pick, xf * far, 1, 1)[0:heads, :])
    both = jnp.sum((incoming * future).reshape(16, 8, width), axis=0)
    cross = keep * jnp.sum(mm_exact(pick, both, 1, 1), axis=1, keepdims=True)[0:heads, :]
    ql = jnp.concatenate(ql_rows, axis=1) * dt
    qs = jnp.concatenate(qs_rows, axis=1) * dt
    pt = jnp.concatenate(p_rows, axis=1)
    sg_ref[...] = ql + qs
    diff = pt - ql
    d_in = running_sums(diff)
    q_in = running_sums(qs)
    d_tot = [d[:, CHUNK - 1:CHUNK] for d in d_in]
    later = jnp.zeros((heads, 1), F32)
    tails = [None] * chunks
    for q in range(chunks - 1, -1, -1):
        span = slice(q * CHUNK, (q + 1) * CHUNK)
        later = later + d_tot[q]
        tails[q] = later - d_in[q] + diff[:, span]
    before = cross
    for q in range(chunks):
        span = slice(q * CHUNK, (q + 1) * CHUNK)
        total = tails[q] + before + q_in[q] - qs[:, span]
        dg_ref[:, span] = ld[:, span] * total
        before = before + q_in[q][:, CHUNK - 1:CHUNK]


def add_heads(in_ref, w_ref, r_ref):
    total = jnp.sum(in_ref[...], axis=0)
    share = w_ref.shape[0]
    w_ref[...] = total[0:share, :]
    r_ref[...] = total[share:2 * share, :]


def call(kernel, outs, args, name, flops=0, seconds_bytes=0):
    smem = pl.BlockSpec(memory_space=pltpu.SMEM)
    vmem = pl.BlockSpec(memory_space=pltpu.VMEM)
    return pl.pallas_call(
        kernel,
        out_shape=outs,
        in_specs=[smem if a.dtype == jnp.int32 else vmem for a in args],
        out_specs=jax.tree.map(lambda _: vmem, outs),
        compiler_params=pltpu.CompilerParams(vmem_limit_bytes=40 * 1024 * 1024),
        cost_estimate=pl.CostEstimate(flops=flops, bytes_accessed=seconds_bytes, transcendentals=0),
        name=name,
    )(*args)


def shards(inputs, write_map, read_map, step_scale, log_decay, lengths, out_grad):
    steps, width = inputs.shape
    heads = step_scale.shape[0]
    state = write_map.shape[1]
    blocks = lax.axis_size("ctx")
    groups = lax.axis_size("head")
    share = steps // groups
    sds = jax.ShapeDtypeStruct
    offset = (lax.axis_index("ctx") * steps).astype(jnp.int32).reshape(1)
    common = (lengths, offset, log_decay, step_scale, write_map, read_map, inputs, out_grad)
    pay = call(state_terms, sds((blocks * 16, 128), F32), common, "state_terms", 200_000_000, 2_000_000)
    got = lax.all_to_all(pay.reshape(blocks, 16, 128), "ctx", 0, 0)
    y, p, wl, rl, xh, xl, gh, gl = call(
        local_part,
        [sds((steps, width), F32), sds((steps, width), F32), sds((steps, state), F32), sds((steps, state), F32)]
        + [sds((steps, width), BF16)] * 4,
        common, "local_part", 4_000_000_000, 20_000_000)
    scanned = call(scan_blocks, sds((blocks * 8, 128), F32), (got.reshape(blocks * 16, 128),), "scan_blocks", 1_000_000, 1_000_000)
    states = lax.all_to_all(scanned.reshape(blocks, 8, 128), "ctx", 0, 0).reshape(blocks * 8, 128)
    terms = call(shared_grads, sds((groups, 2 * share, state), F32), (states, wl, rl, xh, xl, gh, gl),
                 "shared_grads", 200_000_000, 2_000_000)
    summed = lax.all_to_all(terms, "head", 0, 0)
    outputs, input_grad, step_grad, decay_grad = call(
        finish,
        [sds((steps, width), BF16), sds((steps, width), BF16), sds((heads, steps), F32), sds((heads, steps), F32)],
        common + (y, p, states), "finish", 4_000_000_000, 20_000_000)
    write_grad, read_grad = call(
        add_heads, [sds((share, state), F32), sds((share, state), F32)], (summed,), "add_heads", 1_000_000, 1_000_000)
    return (outputs, input_grad, write_grad, read_grad, step_grad, decay_grad)


def solution(mesh):
    placed = (
        P("ctx", "head"),
        P("ctx", None),
        P("ctx", None),
        P("head", "ctx"),
        P("head", "ctx"),
        P(),
        P("ctx", "head"),
    )
    return jax.shard_map(
        shards,
        mesh=mesh,
        in_specs=placed,
        out_specs=(
            P("ctx", "head"),
            P("ctx", "head"),
            P(("ctx", "head"), None),
            P(("ctx", "head"), None),
            P("head", "ctx"),
            P("head", "ctx"),
        ),
        check_vma=False,
    )
```

```python
import jax
import jax.numpy as jnp
from jax import lax
from jax.experimental import pallas as pl
from jax.experimental.pallas import tpu as pltpu
from jax.sharding import PartitionSpec as P

F32 = jnp.float32
BF16 = jnp.bfloat16
CHUNK = 128
NEG = -1e30
PIECE = 9


def split(v):
    hi = v.astype(BF16)
    return hi, (v - hi.astype(F32)).astype(BF16)


def mm(a, b, ca, cb):
    return lax.dot_general(a, b, (((ca,), (cb,)), ((), ())), preferred_element_type=F32)


def mm_exact(a, b, ca, cb):
    return lax.dot_general(
        a, b, (((ca,), (cb,)), ((), ())),
        precision=lax.Precision.HIGHEST, preferred_element_type=F32,
    )


def iota(shape, dim):
    return lax.broadcasted_iota(jnp.int32, shape, dim)


def records_at(len_ref, pos):
    start = jnp.int32(0)
    total = (pos >= start).astype(jnp.int32)
    for k in range(len_ref.shape[0] - 1):
        start = start + len_ref[k]
        total = total + (pos >= start).astype(jnp.int32)
    return total


def scalar_record(len_ref, pos):
    start = jnp.int32(0)
    total = jnp.where(pos >= start, 1, 0)
    for k in range(len_ref.shape[0] - 1):
        start = start + len_ref[k]
        total = total + jnp.where(pos >= start, 1, 0)
    return total


def running_sums(rows):
    heads, steps = rows.shape
    chunks = steps // CHUNK
    stacked = jnp.concatenate([rows[:, q * CHUNK:(q + 1) * CHUNK] for q in range(chunks)], axis=0)
    tri = (iota((CHUNK, CHUNK), 0) <= iota((CHUNK, CHUNK), 1)).astype(F32)
    sums = mm_exact(stacked, tri, 1, 0)
    return [sums[q * heads:(q + 1) * heads, :] for q in range(chunks)]


def block_rows(len_ref, offset, ld, dt):
    heads, steps = ld.shape
    parts = running_sums(ld)
    total = jnp.zeros((heads, 1), F32)
    cums = []
    for part in parts:
        cums.append(part + total)
        total = total + part[:, CHUNK - 1:CHUNK]
    cum = jnp.concatenate(cums, axis=1)
    rec = records_at(len_ref, offset + iota((1, steps), 1))
    last = scalar_record(len_ref, offset + steps - 1)
    prev = scalar_record(len_ref, offset - 1)
    enter = jnp.exp(jnp.where(rec == prev, cum, NEG))
    leave = jnp.exp(jnp.where(rec == last, total - cum, NEG))
    keep = jnp.exp(jnp.where(last == prev, total, NEG))
    return enter, leave, keep


def lanes_of(cols, first, heads):
    rows = cols.shape[0]
    low = iota((rows, 128), 1) < 64
    out = []
    for h in range(0, heads, 2):
        a = cols[:, first + h:first + h + 1]
        b = cols[:, first + h + 1:first + h + 2]
        out.append(jnp.where(low, a, b))
    return jnp.concatenate(out, axis=1)


def state_terms(len_ref, off_ref, ld_hbm, dt_hbm, w_hbm, r_hbm, x_hbm, g_hbm, pay_ref,
                ld_ref, dt_ref, w_ref, r_ref, x_ref, g_ref, sems):
    copies = [
        pltpu.make_async_copy(src, dst, sems.at[i])
        for i, (src, dst) in enumerate((
            (ld_hbm, ld_ref), (dt_hbm, dt_ref), (x_hbm, x_ref),
            (w_hbm, w_ref), (g_hbm, g_ref), (r_hbm, r_ref)))
    ]
    for copy in copies:
        copy.start()
    copies[0].wait()
    copies[1].wait()
    heads, steps = ld_ref.shape
    offset = off_ref[0]
    dt = dt_ref[...]
    enter, leave, keep = block_rows(len_ref, offset, ld_ref[...], dt)
    stack = jnp.concatenate([leave * dt, enter], axis=0)
    cols = [jnp.transpose(stack[:, q * CHUNK:(q + 1) * CHUNK]) for q in range(steps // CHUNK)]

    def scaled(ref, first):
        return split(jnp.concatenate([
            ref[pl.ds(q * CHUNK, CHUNK), :].astype(F32) * lanes_of(cols[q], first, heads)
            for q in range(steps // CHUNK)], axis=0))

    for copy in copies[2:]:
        copy.wait()
    x_hi, x_lo = scaled(x_ref, 0)
    w = w_ref[...]
    fresh = mm(w, x_hi, 0, 0) + mm(w, x_lo, 0, 0)
    g_hi, g_lo = scaled(g_ref, heads)
    r = r_ref[...]
    back = mm(r, g_hi, 0, 0) + mm(r, g_lo, 0, 0)
    low = iota((32, 128), 1) < 64
    for half in range(2):
        lanes = slice(128 * half, 128 * half + 128)
        base = 32 * PIECE * half
        for i in range(4):
            rows = slice(32 * i, 32 * i + 32)
            pay_ref[pl.ds(base + i, 32, stride=PIECE), :] = fresh[rows, lanes]
            pay_ref[pl.ds(base + 4 + i, 32, stride=PIECE), :] = back[rows, lanes]
        pair = jnp.where(low, keep[2 * half:2 * half + 1, :], keep[2 * half + 1:2 * half + 2, :])
        pay_ref[pl.ds(base + 8, 32, stride=PIECE), :] = pair


def scan_blocks(in_ref, out_ref):
    blocks = in_ref.shape[0] // PIECE
    forward = iota((8, 128), 0) < 4
    carry = jnp.zeros((8, 128), F32)
    held = []
    for j in range(blocks):
        held.append(carry)
        carry = carry * in_ref[PIECE * j + 8:PIECE * j + 9, :] + in_ref[PIECE * j:PIECE * j + 8, :]
    carry = jnp.zeros((8, 128), F32)
    for j in range(blocks - 1, -1, -1):
        out_ref[8 * j:8 * j + 8, :] = jnp.where(forward, held[j], carry)
        carry = carry * in_ref[PIECE * j + 8:PIECE * j + 9, :] + in_ref[PIECE * j:PIECE * j + 8, :]


def read_states(st_ref):
    both = []
    for kind in range(2):
        halves = []
        for half in range(2):
            halves.append(jnp.concatenate(
                [st_ref[pl.ds(256 * half + 4 * kind + i, 32, stride=8), :] for i in range(4)],
                axis=0))
        both.append(jnp.concatenate(halves, axis=1))
    return both


def local_part(len_ref, off_ref, ld_ref, dt_ref, w_ref, r_ref, x_ref, g_ref,
               y_ref, p_ref, wl_ref, rl_ref, xh_ref, xl_ref, gh_ref, gl_ref):
    heads, steps = ld_ref.shape
    chunks = steps // CHUNK
    offset = off_ref[0]
    ld = ld_ref[...]
    dt_all = dt_ref[...]
    enter_b, leave_b, _ = block_rows(len_ref, offset, ld, dt_all)
    parts = running_sums(ld)
    low = iota((CHUNK, 128), 1) < 64
    causal = iota((CHUNK, CHUNK), 1) <= iota((CHUNK, CHUNK), 0)
    saved = []
    for q in range(chunks):
        rows = pl.ds(q * CHUNK, CHUNK)
        span = slice(q * CHUNK, (q + 1) * CHUNK)
        first = offset + q * CHUNK
        cum = parts[q]
        total = cum[:, CHUNK - 1:CHUNK]
        dt = dt_all[:, span]
        rec_row = records_at(len_ref, first + iota((1, CHUNK), 1))
        rec_col = records_at(len_ref, first + iota((CHUNK, 1), 0))
        last = scalar_record(len_ref, first + CHUNK - 1)
        prev = scalar_record(len_ref, first - 1)
        enter = jnp.exp(jnp.where(rec_row == prev, cum, NEG))
        leave = jnp.exp(jnp.where(rec_row == last, total - cum, NEG))
        keep = jnp.exp(jnp.where(last == prev, total, NEG))
        stack = jnp.concatenate(
            [cum, enter, leave, leave * dt, leave_b[:, span] * dt, enter_b[:, span]], axis=0)
        cols = jnp.transpose(stack)
        x = x_ref[rows, :]
        g = g_ref[rows, :]
        xf = x.astype(F32)
        gf = g.astype(F32)
        xb_hi, xb_lo = split(xf * lanes_of(cols, 4 * heads, heads))
        gb_hi, gb_lo = split(gf * lanes_of(cols, 5 * heads, heads))
        xh_ref[rows, :] = xb_hi
        xl_ref[rows, :] = xb_lo
        gh_ref[rows, :] = gb_hi
        gl_ref[rows, :] = gb_lo
        enter_lanes = lanes_of(cols, heads, heads)
        leave_lanes = lanes_of(cols, 2 * heads, heads)
        xc = split(xf * lanes_of(cols, 3 * heads, heads))
        gc = split(gf * enter_lanes)
        w = w_ref[rows, :]
        r = r_ref[rows, :]
        fresh = mm(w, xc[0], 0, 0) + mm(w, xc[1], 0, 0)
        back = mm(r, gc[0], 0, 0) + mm(r, gc[1], 0, 0)
        keep_row = jnp.concatenate([
            jnp.where(iota((1, 128), 1) < 64, keep[h:h + 1, :], keep[h + 1:h + 2, :])
            for h in range(0, heads, 2)], axis=1)
        inside = causal & (rec_row == rec_col)
        scores = mm(r, w, 1, 1)
        total_e = jnp.zeros((CHUNK, CHUNK), F32)
        y_parts, p_parts = [], []
        for h in range(heads):
            pair = slice(128 * (h // 2), 128 * (h // 2) + 128)
            x_pair = x[:, pair]
            g_pair = g[:, pair]
            mine = low if h % 2 == 0 else ~low
            decays = jnp.exp(jnp.where(inside, cols[:, h:h + 1] - cum[h:h + 1, :], NEG))
            weighted = scores * decays
            dt_row = dt[h:h + 1, :]
            a_hi, a_lo = split(weighted * dt_row)
            y_parts.append(mm(a_hi, x_pair, 1, 0) + mm(a_lo, x_pair, 1, 0))
            b_hi, b_lo = split(weighted)
            p_parts.append(mm(b_hi, g_pair, 0, 0) + mm(b_lo, g_pair, 0, 0))
            g_mine = jnp.where(mine, gf[:, pair], 0.0).astype(BF16)
            total_e = total_e + decays * dt_row * mm(g_mine, x_pair, 1, 1)
        y = jnp.concatenate([jnp.where(low, y_parts[h], y_parts[h + 1]) for h in range(0, heads, 2)], axis=1)
        p = jnp.concatenate([jnp.where(low, p_parts[h], p_parts[h + 1]) for h in range(0, heads, 2)], axis=1)
        e_hi, e_lo = split(total_e)
        wl = mm(e_hi, r, 0, 0) + mm(e_lo, r, 0, 0)
        rl = mm(e_hi, w, 1, 0) + mm(e_lo, w, 1, 0)
        saved.append((rows, y, p, wl, rl, xc, gc, w, r, fresh, back, keep_row, enter_lanes, leave_lanes))
    state = None
    for q in range(chunks):
        rows, y, p, wl, rl, xc, gc, w, r, fresh, back, keep_row, enter_lanes, leave_lanes = saved[q]
        if state is not None:
            s_hi, s_lo = split(state)
            y = y + enter_lanes * (mm(r, s_hi, 1, 0) + mm(r, s_lo, 1, 0))
            rl = rl + (mm(gc[0], s_hi, 1, 1) + mm(gc[0], s_lo, 1, 1) + mm(gc[1], s_hi, 1, 1))
            state = state * keep_row + fresh
        else:
            state = fresh
        y_ref[rows, :] = y
        rl_ref[rows, :] = rl
    future = None
    for q in range(chunks - 1, -1, -1):
        rows, y, p, wl, rl, xc, gc, w, r, fresh, back, keep_row, enter_lanes, leave_lanes = saved[q]
        if future is not None:
            f_hi, f_lo = split(future)
            p = p + leave_lanes * (mm(w, f_hi, 1, 0) + mm(w, f_lo, 1, 0))
            wl = wl + (mm(xc[0], f_hi, 1, 1) + mm(xc[0], f_lo, 1, 1) + mm(xc[1], f_hi, 1, 1))
            future = future * keep_row + back
        else:
            future = back
        p_ref[rows, :] = p
        wl_ref[rows, :] = wl


def shared_grads(st_ref, wl_ref, rl_ref, xh_ref, xl_ref, gh_ref, gl_ref, out_ref):
    steps = wl_ref.shape[0]
    incoming, future = read_states(st_ref)
    s_hi, s_lo = split(incoming)
    f_hi, f_lo = split(future)
    xh = xh_ref[...]
    gh = gh_ref[...]
    w = wl_ref[...] + mm(xh, f_hi, 1, 1) + mm(xh, f_lo, 1, 1) + mm(xl_ref[...], f_hi, 1, 1)
    r = rl_ref[...] + mm(gh, s_hi, 1, 1) + mm(gh, s_lo, 1, 1) + mm(gl_ref[...], s_hi, 1, 1)
    share = steps // out_ref.shape[0]
    out_ref[:, 0:share, :] = w.reshape(out_ref.shape[0], share, w.shape[1])
    out_ref[:, share:2 * share, :] = r.reshape(out_ref.shape[0], share, r.shape[1])


def finish(len_ref, off_ref, ld_ref, dt_ref, w_ref, r_ref, x_ref, g_ref, y_ref, p_ref, st_ref,
           out_ref, xg_ref, sg_ref, dg_ref):
    heads, steps = ld_ref.shape
    chunks = steps // CHUNK
    offset = off_ref[0]
    ld = ld_ref[...]
    dt = dt_ref[...]
    enter, leave, keep = block_rows(len_ref, offset, ld, dt)
    incoming, future = read_states(st_ref)
    s_hi, s_lo = split(incoming)
    f_hi, f_lo = split(future)
    width = x_ref.shape[1]
    pick = (iota((8, width), 1) // 64 == iota((8, width), 0)).astype(F32)
    stack = jnp.concatenate([enter, leave, dt, dt], axis=0)
    p_rows, ql_rows, qs_rows = [], [], []
    for q in range(chunks):
        rows = pl.ds(q * CHUNK, CHUNK)
        cols = jnp.transpose(stack[:, q * CHUNK:(q + 1) * CHUNK])
        r = r_ref[rows, :]
        w = w_ref[rows, :]
        y = y_ref[rows, :] + lanes_of(cols, 0, heads) * (mm(r, s_hi, 1, 0) + mm(r, s_lo, 1, 0))
        near = p_ref[rows, :]
        far = lanes_of(cols, heads, heads) * (mm(w, f_hi, 1, 0) + mm(w, f_lo, 1, 0))
        out_ref[rows, :] = y.astype(BF16)
        xg_ref[rows, :] = (lanes_of(cols, 2 * heads, heads) * (near + far)).astype(BF16)
        xf = x_ref[rows, :].astype(F32)
        p_rows.append(mm_exact(pick, g_ref[rows, :].astype(F32) * y, 1, 1)[0:heads, :])
        ql_rows.append(mm_exact(pick, xf * near, 1, 1)[0:heads, :])
        qs_rows.append(mm_exact(pick, xf * far, 1, 1)[0:heads, :])
    both = jnp.sum((incoming * future).reshape(16, 8, width), axis=0)
    cross = keep * jnp.sum(mm_exact(pick, both, 1, 1), axis=1, keepdims=True)[0:heads, :]
    ql = jnp.concatenate(ql_rows, axis=1) * dt
    qs = jnp.concatenate(qs_rows, axis=1) * dt
    pt = jnp.concatenate(p_rows, axis=1)
    sg_ref[...] = ql + qs
    diff = pt - ql
    d_in = running_sums(diff)
    q_in = running_sums(qs)
    d_tot = [d[:, CHUNK - 1:CHUNK] for d in d_in]
    later = jnp.zeros((heads, 1), F32)
    tails = [None] * chunks
    for q in range(chunks - 1, -1, -1):
        span = slice(q * CHUNK, (q + 1) * CHUNK)
        later = later + d_tot[q]
        tails[q] = later - d_in[q] + diff[:, span]
    before = cross
    for q in range(chunks):
        span = slice(q * CHUNK, (q + 1) * CHUNK)
        total = tails[q] + before + q_in[q] - qs[:, span]
        dg_ref[:, span] = ld[:, span] * total
        before = before + q_in[q][:, CHUNK - 1:CHUNK]


def add_heads(in_ref, w_ref, r_ref):
    total = jnp.sum(in_ref[...], axis=0)
    share = w_ref.shape[0]
    w_ref[...] = total[0:share, :]
    r_ref[...] = total[share:2 * share, :]


def call(kernel, outs, args, name, flops=0, moved=0, scratch=(), fetched=False, limit=40):
    smem = pl.BlockSpec(memory_space=pltpu.SMEM)
    vmem = pl.BlockSpec(memory_space=pltpu.VMEM)
    big = pl.BlockSpec(memory_space=pltpu.HBM) if fetched else vmem
    return pl.pallas_call(
        kernel,
        out_shape=outs,
        in_specs=[smem if a.dtype == jnp.int32 else big for a in args],
        out_specs=jax.tree.map(lambda _: vmem, outs),
        scratch_shapes=list(scratch),
        compiler_params=pltpu.CompilerParams(vmem_limit_bytes=limit * 1024 * 1024),
        cost_estimate=pl.CostEstimate(flops=flops, bytes_accessed=moved, transcendentals=0),
        name=name,
    )(*args)


def shards(inputs, write_map, read_map, step_scale, log_decay, lengths, out_grad):
    steps, width = inputs.shape
    heads = step_scale.shape[0]
    state = write_map.shape[1]
    blocks = lax.axis_size("ctx")
    groups = lax.axis_size("head")
    share = steps // groups
    sds = jax.ShapeDtypeStruct
    offset = (lax.axis_index("ctx") * steps).astype(jnp.int32).reshape(1)
    common = (lengths, offset, log_decay, step_scale, write_map, read_map, inputs, out_grad)
    buffers = [pltpu.VMEM(a.shape, a.dtype) for a in common[2:]] + [pltpu.SemaphoreType.DMA((6,))]
    pay = call(state_terms, sds((blocks * PIECE, 128), F32), common, "state_terms", 200_000_000, 2_000_000,
               buffers, True, 60)
    got = lax.all_to_all(pay.reshape(blocks, 1, PIECE * 128), "ctx", 0, 0)
    y, p, wl, rl, xh, xl, gh, gl = call(
        local_part,
        [sds((steps, width), F32), sds((steps, width), F32), sds((steps, state), F32), sds((steps, state), F32)]
        + [sds((steps, width), BF16)] * 4,
        common, "local_part", 4_000_000_000, 20_000_000)
    scanned = call(scan_blocks, sds((blocks * 8, 128), F32), (got.reshape(blocks * PIECE, 128),), "scan_blocks", 1_000_000, 1_000_000)
    states = lax.all_to_all(scanned.reshape(blocks, 8, 128), "ctx", 0, 0).reshape(blocks * 8, 128)
    terms = call(shared_grads, sds((groups, 2 * share, state), F32), (states, wl, rl, xh, xl, gh, gl),
                 "shared_grads", 200_000_000, 2_000_000)
    summed = lax.all_to_all(terms, "head", 0, 0)
    outputs, input_grad, step_grad, decay_grad = call(
        finish,
        [sds((steps, width), BF16), sds((steps, width), BF16), sds((heads, steps), F32), sds((heads, steps), F32)],
        common + (y, p, states), "finish", 4_000_000_000, 20_000_000)
    write_grad, read_grad = call(
        add_heads, [sds((share, state), F32), sds((share, state), F32)], (summed,), "add_heads", 1_000_000, 1_000_000)
    return (outputs, input_grad, write_grad, read_grad, step_grad, decay_grad)


def solution(mesh):
    placed = (
        P("ctx", "head"),
        P("ctx", None),
        P("ctx", None),
        P("head", "ctx"),
        P("head", "ctx"),
        P(),
        P("ctx", "head"),
    )
    return jax.shard_map(
        shards,
        mesh=mesh,
        in_specs=placed,
        out_specs=(
            P("ctx", "head"),
            P("ctx", "head"),
            P(("ctx", "head"), None),
            P(("ctx", "head"), None),
            P("head", "ctx"),
            P("head", "ctx"),
        ),
        check_vma=False,
    )
```

```python
import jax
import jax.numpy as jnp
from jax import lax
from jax.experimental import pallas as pl
from jax.experimental.pallas import tpu as pltpu
from jax.sharding import PartitionSpec as P

F32 = jnp.float32
BF16 = jnp.bfloat16
CHUNK = 128
NEG = -1e30
PIECE = 9


def split(v):
    hi = v.astype(BF16)
    return hi, (v - hi.astype(F32)).astype(BF16)


def mm(a, b, ca, cb):
    return lax.dot_general(a, b, (((ca,), (cb,)), ((), ())), preferred_element_type=F32)


def mm_exact(a, b, ca, cb):
    return lax.dot_general(
        a, b, (((ca,), (cb,)), ((), ())),
        precision=lax.Precision.HIGHEST, preferred_element_type=F32,
    )


def iota(shape, dim):
    return lax.broadcasted_iota(jnp.int32, shape, dim)


def records_at(len_ref, pos):
    start = jnp.int32(0)
    total = (pos >= start).astype(jnp.int32)
    for k in range(len_ref.shape[0] - 1):
        start = start + len_ref[k]
        total = total + (pos >= start).astype(jnp.int32)
    return total


def scalar_record(len_ref, pos):
    start = jnp.int32(0)
    total = jnp.where(pos >= start, 1, 0)
    for k in range(len_ref.shape[0] - 1):
        start = start + len_ref[k]
        total = total + jnp.where(pos >= start, 1, 0)
    return total


def running_sums(rows):
    heads, steps = rows.shape
    chunks = steps // CHUNK
    stacked = jnp.concatenate([rows[:, q * CHUNK:(q + 1) * CHUNK] for q in range(chunks)], axis=0)
    tri = (iota((CHUNK, CHUNK), 0) <= iota((CHUNK, CHUNK), 1)).astype(F32)
    sums = mm_exact(stacked, tri, 1, 0)
    return [sums[q * heads:(q + 1) * heads, :] for q in range(chunks)]


def block_rows(len_ref, offset, ld, dt):
    heads, steps = ld.shape
    parts = running_sums(ld)
    total = jnp.zeros((heads, 1), F32)
    cums = []
    for part in parts:
        cums.append(part + total)
        total = total + part[:, CHUNK - 1:CHUNK]
    cum = jnp.concatenate(cums, axis=1)
    rec = records_at(len_ref, offset + iota((1, steps), 1))
    last = scalar_record(len_ref, offset + steps - 1)
    prev = scalar_record(len_ref, offset - 1)
    enter = jnp.exp(jnp.where(rec == prev, cum, NEG))
    leave = jnp.exp(jnp.where(rec == last, total - cum, NEG))
    keep = jnp.exp(jnp.where(last == prev, total, NEG))
    return enter, leave, keep


def lanes_of(cols, first, heads):
    rows = cols.shape[0]
    low = iota((rows, 128), 1) < 64
    out = []
    for h in range(0, heads, 2):
        a = cols[:, first + h:first + h + 1]
        b = cols[:, first + h + 1:first + h + 2]
        out.append(jnp.where(low, a, b))
    return jnp.concatenate(out, axis=1)


def block_start(steps):
    return lax.axis_index("ctx") * steps


def state_terms(len_hbm, ld_hbm, dt_hbm, w_hbm, r_hbm, x_hbm, g_hbm, pay_hbm,
                len_ref, ld_ref, dt_ref, w_ref, r_ref, x_ref, g_ref, pay_ref, sems):
    pairs = ((len_hbm, len_ref), (ld_hbm, ld_ref), (dt_hbm, dt_ref), (x_hbm, x_ref),
             (w_hbm, w_ref), (g_hbm, g_ref), (r_hbm, r_ref))
    copies = [pltpu.make_async_copy(src, dst, sems.at[i]) for i, (src, dst) in enumerate(pairs)]
    for copy in copies:
        copy.start()
    for copy in copies[:3]:
        copy.wait()
    heads, steps = ld_ref.shape
    dt = dt_ref[...]
    enter, leave, keep = block_rows(len_ref, block_start(steps), ld_ref[...], dt)
    stack = jnp.concatenate([leave * dt, enter], axis=0)
    cols = [jnp.transpose(stack[:, q * CHUNK:(q + 1) * CHUNK]) for q in range(steps // CHUNK)]
    low = iota((CHUNK, 128), 1) < 64

    def scaled(ref, lanes, first):
        return split(jnp.concatenate([
            ref[pl.ds(q * CHUNK, CHUNK), lanes].astype(F32)
            * jnp.where(low, cols[q][:, first:first + 1], cols[q][:, first + 1:first + 2])
            for q in range(steps // CHUNK)], axis=0))

    for copy in copies[3:]:
        copy.wait()
    w = w_ref[...]
    r = r_ref[...]
    half_rows = pay_ref.shape[0] // 2
    sends = []
    for half in range(2):
        lanes = slice(128 * half, 128 * half + 128)
        base = half_rows * half
        x_hi, x_lo = scaled(x_ref, lanes, 2 * half)
        fresh = mm(w, x_hi, 0, 0) + mm(w, x_lo, 0, 0)
        g_hi, g_lo = scaled(g_ref, lanes, heads + 2 * half)
        back = mm(r, g_hi, 0, 0) + mm(r, g_lo, 0, 0)
        for i in range(4):
            rows = slice(32 * i, 32 * i + 32)
            pay_ref[pl.ds(base + i, 32, stride=PIECE), :] = fresh[rows]
            pay_ref[pl.ds(base + 4 + i, 32, stride=PIECE), :] = back[rows]
        pair = jnp.where(low[0:32], keep[2 * half:2 * half + 1, :], keep[2 * half + 1:2 * half + 2, :])
        pay_ref[pl.ds(base + 8, 32, stride=PIECE), :] = pair
        span = pl.ds(base, half_rows)
        sends.append(pltpu.make_async_copy(pay_ref.at[span], pay_hbm.at[span], sems.at[len(pairs) + half]))
        sends[-1].start()
    for send in sends:
        send.wait()


def scan_blocks(in_ref, out_ref):
    blocks = in_ref.shape[0] // PIECE
    forward = iota((8, 128), 0) < 4
    carry = jnp.zeros((8, 128), F32)
    held = []
    for j in range(blocks):
        held.append(carry)
        carry = carry * in_ref[PIECE * j + 8:PIECE * j + 9, :] + in_ref[PIECE * j:PIECE * j + 8, :]
    carry = jnp.zeros((8, 128), F32)
    for j in range(blocks - 1, -1, -1):
        out_ref[8 * j:8 * j + 8, :] = jnp.where(forward, held[j], carry)
        carry = carry * in_ref[PIECE * j + 8:PIECE * j + 9, :] + in_ref[PIECE * j:PIECE * j + 8, :]


def read_states(st_ref):
    both = []
    for kind in range(2):
        halves = []
        for half in range(2):
            halves.append(jnp.concatenate(
                [st_ref[pl.ds(256 * half + 4 * kind + i, 32, stride=8), :] for i in range(4)],
                axis=0))
        both.append(jnp.concatenate(halves, axis=1))
    return both


def local_part(len_ref, ld_ref, dt_ref, w_ref, r_ref, x_ref, g_ref,
               y_ref, p_ref, wl_ref, rl_ref, xh_ref, xl_ref, gh_ref, gl_ref):
    heads, steps = ld_ref.shape
    chunks = steps // CHUNK
    offset = block_start(steps)
    ld = ld_ref[...]
    dt_all = dt_ref[...]
    enter_b, leave_b, _ = block_rows(len_ref, offset, ld, dt_all)
    parts = running_sums(ld)
    low = iota((CHUNK, 128), 1) < 64
    causal = iota((CHUNK, CHUNK), 1) <= iota((CHUNK, CHUNK), 0)
    saved = []
    for q in range(chunks):
        rows = pl.ds(q * CHUNK, CHUNK)
        span = slice(q * CHUNK, (q + 1) * CHUNK)
        first = offset + q * CHUNK
        cum = parts[q]
        total = cum[:, CHUNK - 1:CHUNK]
        dt = dt_all[:, span]
        rec_row = records_at(len_ref, first + iota((1, CHUNK), 1))
        rec_col = records_at(len_ref, first + iota((CHUNK, 1), 0))
        last = scalar_record(len_ref, first + CHUNK - 1)
        prev = scalar_record(len_ref, first - 1)
        enter = jnp.exp(jnp.where(rec_row == prev, cum, NEG))
        leave = jnp.exp(jnp.where(rec_row == last, total - cum, NEG))
        keep = jnp.exp(jnp.where(last == prev, total, NEG))
        stack = jnp.concatenate(
            [cum, enter, leave, leave * dt, leave_b[:, span] * dt, enter_b[:, span]], axis=0)
        cols = jnp.transpose(stack)
        x = x_ref[rows, :]
        g = g_ref[rows, :]
        xf = x.astype(F32)
        gf = g.astype(F32)
        xb_hi, xb_lo = split(xf * lanes_of(cols, 4 * heads, heads))
        gb_hi, gb_lo = split(gf * lanes_of(cols, 5 * heads, heads))
        xh_ref[rows, :] = xb_hi
        xl_ref[rows, :] = xb_lo
        gh_ref[rows, :] = gb_hi
        gl_ref[rows, :] = gb_lo
        enter_lanes = lanes_of(cols, heads, heads)
        leave_lanes = lanes_of(cols, 2 * heads, heads)
        xc = split(xf * lanes_of(cols, 3 * heads, heads))
        gc = split(gf * enter_lanes)
        w = w_ref[rows, :]
        r = r_ref[rows, :]
        fresh = mm(w, xc[0], 0, 0) + mm(w, xc[1], 0, 0)
        back = mm(r, gc[0], 0, 0) + mm(r, gc[1], 0, 0)
        keep_row = jnp.concatenate([
            jnp.where(iota((1, 128), 1) < 64, keep[h:h + 1, :], keep[h + 1:h + 2, :])
            for h in range(0, heads, 2)], axis=1)
        inside = causal & (rec_row == rec_col)
        scores = mm(r, w, 1, 1)
        total_e = jnp.zeros((CHUNK, CHUNK), F32)
        y_parts, p_parts = [], []
        for h in range(heads):
            pair = slice(128 * (h // 2), 128 * (h // 2) + 128)
            x_pair = x[:, pair]
            g_pair = g[:, pair]
            mine = low if h % 2 == 0 else ~low
            decays = jnp.exp(jnp.where(inside, cols[:, h:h + 1] - cum[h:h + 1, :], NEG))
            weighted = scores * decays
            dt_row = dt[h:h + 1, :]
            a_hi, a_lo = split(weighted * dt_row)
            y_parts.append(mm(a_hi, x_pair, 1, 0) + mm(a_lo, x_pair, 1, 0))
            b_hi, b_lo = split(weighted)
            p_parts.append(mm(b_hi, g_pair, 0, 0) + mm(b_lo, g_pair, 0, 0))
            g_mine = jnp.where(mine, gf[:, pair], 0.0).astype(BF16)
            total_e = total_e + decays * dt_row * mm(g_mine, x_pair, 1, 1)
        y = jnp.concatenate([jnp.where(low, y_parts[h], y_parts[h + 1]) for h in range(0, heads, 2)], axis=1)
        p = jnp.concatenate([jnp.where(low, p_parts[h], p_parts[h + 1]) for h in range(0, heads, 2)], axis=1)
        e_hi, e_lo = split(total_e)
        wl = mm(e_hi, r, 0, 0) + mm(e_lo, r, 0, 0)
        rl = mm(e_hi, w, 1, 0) + mm(e_lo, w, 1, 0)
        saved.append((rows, y, p, wl, rl, xc, gc, w, r, fresh, back, keep_row, enter_lanes, leave_lanes))
    state = None
    for q in range(chunks):
        rows, y, p, wl, rl, xc, gc, w, r, fresh, back, keep_row, enter_lanes, leave_lanes = saved[q]
        if state is not None:
            s_hi, s_lo = split(state)
            y = y + enter_lanes * (mm(r, s_hi, 1, 0) + mm(r, s_lo, 1, 0))
            rl = rl + (mm(gc[0], s_hi, 1, 1) + mm(gc[0], s_lo, 1, 1) + mm(gc[1], s_hi, 1, 1))
            state = state * keep_row + fresh
        else:
            state = fresh
        y_ref[rows, :] = y
        rl_ref[rows, :] = rl
    future = None
    for q in range(chunks - 1, -1, -1):
        rows, y, p, wl, rl, xc, gc, w, r, fresh, back, keep_row, enter_lanes, leave_lanes = saved[q]
        if future is not None:
            f_hi, f_lo = split(future)
            p = p + leave_lanes * (mm(w, f_hi, 1, 0) + mm(w, f_lo, 1, 0))
            wl = wl + (mm(xc[0], f_hi, 1, 1) + mm(xc[0], f_lo, 1, 1) + mm(xc[1], f_hi, 1, 1))
            future = future * keep_row + back
        else:
            future = back
        p_ref[rows, :] = p
        wl_ref[rows, :] = wl


def shared_grads(st_ref, wl_ref, rl_ref, xh_ref, xl_ref, gh_ref, gl_ref, out_ref):
    steps = wl_ref.shape[0]
    incoming, future = read_states(st_ref)
    s_hi, s_lo = split(incoming)
    f_hi, f_lo = split(future)
    xh = xh_ref[...]
    gh = gh_ref[...]
    w = wl_ref[...] + mm(xh, f_hi, 1, 1) + mm(xh, f_lo, 1, 1) + mm(xl_ref[...], f_hi, 1, 1)
    r = rl_ref[...] + mm(gh, s_hi, 1, 1) + mm(gh, s_lo, 1, 1) + mm(gl_ref[...], s_hi, 1, 1)
    share = steps // out_ref.shape[0]
    out_ref[:, 0:share, :] = w.reshape(out_ref.shape[0], share, w.shape[1])
    out_ref[:, share:2 * share, :] = r.reshape(out_ref.shape[0], share, r.shape[1])


def finish(len_ref, ld_ref, dt_ref, w_ref, r_ref, x_ref, g_ref, y_ref, p_ref, st_ref,
           out_ref, xg_ref, sg_ref, dg_ref):
    heads, steps = ld_ref.shape
    chunks = steps // CHUNK
    offset = block_start(steps)
    ld = ld_ref[...]
    dt = dt_ref[...]
    enter, leave, keep = block_rows(len_ref, offset, ld, dt)
    incoming, future = read_states(st_ref)
    s_hi, s_lo = split(incoming)
    f_hi, f_lo = split(future)
    width = x_ref.shape[1]
    pick = (iota((8, width), 1) // 64 == iota((8, width), 0)).astype(F32)
    stack = jnp.concatenate([enter, leave, dt, dt], axis=0)
    p_rows, ql_rows, qs_rows = [], [], []
    for q in range(chunks):
        rows = pl.ds(q * CHUNK, CHUNK)
        cols = jnp.transpose(stack[:, q * CHUNK:(q + 1) * CHUNK])
        r = r_ref[rows, :]
        w = w_ref[rows, :]
        y = y_ref[rows, :] + lanes_of(cols, 0, heads) * (mm(r, s_hi, 1, 0) + mm(r, s_lo, 1, 0))
        near = p_ref[rows, :]
        far = lanes_of(cols, heads, heads) * (mm(w, f_hi, 1, 0) + mm(w, f_lo, 1, 0))
        out_ref[rows, :] = y.astype(BF16)
        xg_ref[rows, :] = (lanes_of(cols, 2 * heads, heads) * (near + far)).astype(BF16)
        xf = x_ref[rows, :].astype(F32)
        p_rows.append(mm_exact(pick, g_ref[rows, :].astype(F32) * y, 1, 1)[0:heads, :])
        ql_rows.append(mm_exact(pick, xf * near, 1, 1)[0:heads, :])
        qs_rows.append(mm_exact(pick, xf * far, 1, 1)[0:heads, :])
    both = jnp.sum((incoming * future).reshape(16, 8, width), axis=0)
    cross = keep * jnp.sum(mm_exact(pick, both, 1, 1), axis=1, keepdims=True)[0:heads, :]
    ql = jnp.concatenate(ql_rows, axis=1) * dt
    qs = jnp.concatenate(qs_rows, axis=1) * dt
    pt = jnp.concatenate(p_rows, axis=1)
    sg_ref[...] = ql + qs
    diff = pt - ql
    d_in = running_sums(diff)
    q_in = running_sums(qs)
    d_tot = [d[:, CHUNK - 1:CHUNK] for d in d_in]
    later = jnp.zeros((heads, 1), F32)
    tails = [None] * chunks
    for q in range(chunks - 1, -1, -1):
        span = slice(q * CHUNK, (q + 1) * CHUNK)
        later = later + d_tot[q]
        tails[q] = later - d_in[q] + diff[:, span]
    before = cross
    for q in range(chunks):
        span = slice(q * CHUNK, (q + 1) * CHUNK)
        total = tails[q] + before + q_in[q] - qs[:, span]
        dg_ref[:, span] = ld[:, span] * total
        before = before + q_in[q][:, CHUNK - 1:CHUNK]


def add_heads(in_ref, w_ref, r_ref):
    total = jnp.sum(in_ref[...], axis=0)
    share = w_ref.shape[0]
    w_ref[...] = total[0:share, :]
    r_ref[...] = total[share:2 * share, :]


def call(kernel, outs, args, name, flops=0, moved=0, scratch=(), fetched=False, limit=40):
    smem = pl.BlockSpec(memory_space=pltpu.SMEM)
    vmem = pl.BlockSpec(memory_space=pltpu.VMEM)
    hbm = pl.BlockSpec(memory_space=pltpu.HBM)
    return pl.pallas_call(
        kernel,
        out_shape=outs,
        in_specs=[hbm if fetched else smem if a.dtype == jnp.int32 else vmem for a in args],
        out_specs=jax.tree.map(lambda _: hbm if fetched else vmem, outs),
        scratch_shapes=list(scratch),
        compiler_params=pltpu.CompilerParams(vmem_limit_bytes=limit * 1024 * 1024),
        cost_estimate=pl.CostEstimate(flops=flops, bytes_accessed=moved, transcendentals=0),
        name=name,
    )(*args)


def state_terms_call(common, blocks):
    out = jax.ShapeDtypeStruct((blocks * PIECE, 128), F32)
    buffers = [pltpu.SMEM(common[0].shape, common[0].dtype)]
    buffers += [pltpu.VMEM(a.shape, a.dtype) for a in common[1:] + (out,)]
    buffers.append(pltpu.SemaphoreType.DMA((9,)))
    return call(state_terms, out, common, "state_terms", 200_000_000, 2_000_000, buffers, True, 60)


def shards(inputs, write_map, read_map, step_scale, log_decay, lengths, out_grad):
    steps, width = inputs.shape
    heads = step_scale.shape[0]
    state = write_map.shape[1]
    blocks = lax.axis_size("ctx")
    groups = lax.axis_size("head")
    share = steps // groups
    sds = jax.ShapeDtypeStruct
    common = (lengths, log_decay, step_scale, write_map, read_map, inputs, out_grad)
    pay = state_terms_call(common, blocks)
    pay, common = lax.optimization_barrier((pay, common))
    got = lax.all_to_all(pay.reshape(blocks, 1, PIECE * 128), "ctx", 0, 0)
    y, p, wl, rl, xh, xl, gh, gl = call(
        local_part,
        [sds((steps, width), F32), sds((steps, width), F32), sds((steps, state), F32), sds((steps, state), F32)]
        + [sds((steps, width), BF16)] * 4,
        common, "local_part", 4_000_000_000, 20_000_000)
    got, wl, rl = lax.optimization_barrier((got, wl, rl))
    scanned = call(scan_blocks, sds((blocks * 8, 128), F32), (got.reshape(blocks * PIECE, 128),), "scan_blocks", 1_000_000, 1_000_000)
    states = lax.all_to_all(scanned.reshape(blocks, 8, 128), "ctx", 0, 0).reshape(blocks * 8, 128)
    terms = call(shared_grads, sds((groups, 2 * share, state), F32), (states, wl, rl, xh, xl, gh, gl),
                 "shared_grads", 200_000_000, 2_000_000)
    summed = lax.all_to_all(terms, "head", 0, 0)
    outputs, input_grad, step_grad, decay_grad = call(
        finish,
        [sds((steps, width), BF16), sds((steps, width), BF16), sds((heads, steps), F32), sds((heads, steps), F32)],
        common + (y, p, states), "finish", 4_000_000_000, 20_000_000)
    write_grad, read_grad = call(
        add_heads, [sds((share, state), F32), sds((share, state), F32)], (summed,), "add_heads", 1_000_000, 1_000_000)
    return (outputs, input_grad, write_grad, read_grad, step_grad, decay_grad)


def solution(mesh):
    placed = (
        P("ctx", "head"),
        P("ctx", None),
        P("ctx", None),
        P("head", "ctx"),
        P("head", "ctx"),
        P(),
        P("ctx", "head"),
    )
    return jax.shard_map(
        shards,
        mesh=mesh,
        in_specs=placed,
        out_specs=(
            P("ctx", "head"),
            P("ctx", "head"),
            P(("ctx", "head"), None),
            P(("ctx", "head"), None),
            P("head", "ctx"),
            P("head", "ctx"),
        ),
        check_vma=False,
    )
```

```python
import functools

import jax
import jax.numpy as jnp
from jax import lax
from jax.experimental import pallas as pl
from jax.experimental.pallas import tpu as pltpu
from jax.sharding import PartitionSpec as P

F32 = jnp.float32
BF16 = jnp.bfloat16
CHUNK = 128
NEG = -1e30
PIECE = 9


def split(v):
    hi = v.astype(BF16)
    return hi, (v - hi.astype(F32)).astype(BF16)


def mm(a, b, ca, cb):
    return lax.dot_general(a, b, (((ca,), (cb,)), ((), ())), preferred_element_type=F32)


def mm_exact(a, b, ca, cb):
    return lax.dot_general(
        a, b, (((ca,), (cb,)), ((), ())),
        precision=lax.Precision.HIGHEST, preferred_element_type=F32,
    )


def iota(shape, dim):
    return lax.broadcasted_iota(jnp.int32, shape, dim)


def records_at(len_ref, pos):
    start = jnp.int32(0)
    total = (pos >= start).astype(jnp.int32)
    for k in range(len_ref.shape[0] - 1):
        start = start + len_ref[k]
        total = total + (pos >= start).astype(jnp.int32)
    return total


def scalar_record(len_ref, pos):
    start = jnp.int32(0)
    total = jnp.where(pos >= start, 1, 0)
    for k in range(len_ref.shape[0] - 1):
        start = start + len_ref[k]
        total = total + jnp.where(pos >= start, 1, 0)
    return total


def running_sums(rows):
    heads, steps = rows.shape
    chunks = steps // CHUNK
    stacked = jnp.concatenate([rows[:, q * CHUNK:(q + 1) * CHUNK] for q in range(chunks)], axis=0)
    tri = (iota((CHUNK, CHUNK), 0) <= iota((CHUNK, CHUNK), 1)).astype(F32)
    sums = mm_exact(stacked, tri, 1, 0)
    return [sums[q * heads:(q + 1) * heads, :] for q in range(chunks)]


def block_rows(len_ref, offset, ld, dt):
    heads, steps = ld.shape
    parts = running_sums(ld)
    total = jnp.zeros((heads, 1), F32)
    cums = []
    for part in parts:
        cums.append(part + total)
        total = total + part[:, CHUNK - 1:CHUNK]
    cum = jnp.concatenate(cums, axis=1)
    rec = records_at(len_ref, offset + iota((1, steps), 1))
    last = scalar_record(len_ref, offset + steps - 1)
    prev = scalar_record(len_ref, offset - 1)
    enter = jnp.exp(jnp.where(rec == prev, cum, NEG))
    leave = jnp.exp(jnp.where(rec == last, total - cum, NEG))
    keep = jnp.exp(jnp.where(last == prev, total, NEG))
    return enter, leave, keep


def lanes_of(cols, first, heads):
    rows = cols.shape[0]
    low = iota((rows, 128), 1) < 64
    out = []
    for h in range(0, heads, 2):
        a = cols[:, first + h:first + h + 1]
        b = cols[:, first + h + 1:first + h + 2]
        out.append(jnp.where(low, a, b))
    return jnp.concatenate(out, axis=1)


def block_start(steps):
    return lax.axis_index("ctx") * steps


def state_terms(len_hbm, ld_hbm, dt_hbm, w_hbm, r_hbm, x_hbm, g_hbm, pay_hbm,
                len_ref, ld_ref, dt_ref, w_ref, r_ref, x_ref, g_ref, pay_ref, sems):
    pairs = ((len_hbm, len_ref), (ld_hbm, ld_ref), (dt_hbm, dt_ref), (x_hbm, x_ref),
             (w_hbm, w_ref), (g_hbm, g_ref), (r_hbm, r_ref))
    copies = [pltpu.make_async_copy(src, dst, sems.at[i]) for i, (src, dst) in enumerate(pairs)]
    for copy in copies:
        copy.start()
    for copy in copies[:3]:
        copy.wait()
    heads, steps = ld_ref.shape
    dt = dt_ref[...]
    enter, leave, keep = block_rows(len_ref, block_start(steps), ld_ref[...], dt)
    stack = jnp.concatenate([leave * dt, enter], axis=0)
    cols = [jnp.transpose(stack[:, q * CHUNK:(q + 1) * CHUNK]) for q in range(steps // CHUNK)]
    low = iota((CHUNK, 128), 1) < 64

    def scaled(ref, lanes, first):
        return split(jnp.concatenate([
            ref[pl.ds(q * CHUNK, CHUNK), lanes].astype(F32)
            * jnp.where(low, cols[q][:, first:first + 1], cols[q][:, first + 1:first + 2])
            for q in range(steps // CHUNK)], axis=0))

    for copy in copies[3:]:
        copy.wait()
    w = w_ref[...]
    r = r_ref[...]
    half_rows = pay_ref.shape[0] // 2
    sends = []
    for half in range(2):
        lanes = slice(128 * half, 128 * half + 128)
        base = half_rows * half
        x_hi, x_lo = scaled(x_ref, lanes, 2 * half)
        fresh = mm(w, x_hi, 0, 0) + mm(w, x_lo, 0, 0)
        g_hi, g_lo = scaled(g_ref, lanes, heads + 2 * half)
        back = mm(r, g_hi, 0, 0) + mm(r, g_lo, 0, 0)
        for i in range(4):
            rows = slice(32 * i, 32 * i + 32)
            pay_ref[pl.ds(base + i, 32, stride=PIECE), :] = fresh[rows]
            pay_ref[pl.ds(base + 4 + i, 32, stride=PIECE), :] = back[rows]
        pair = jnp.where(low[0:32], keep[2 * half:2 * half + 1, :], keep[2 * half + 1:2 * half + 2, :])
        pay_ref[pl.ds(base + 8, 32, stride=PIECE), :] = pair
        span = pl.ds(base, half_rows)
        sends.append(pltpu.make_async_copy(pay_ref.at[span], pay_hbm.at[span], sems.at[len(pairs) + half]))
        sends[-1].start()
    for send in sends:
        send.wait()


def scan_blocks(in_ref, out_ref):
    blocks = in_ref.shape[0] // PIECE
    forward = iota((8, 128), 0) < 4
    carry = jnp.zeros((8, 128), F32)
    held = []
    for j in range(blocks):
        held.append(carry)
        carry = carry * in_ref[PIECE * j + 8:PIECE * j + 9, :] + in_ref[PIECE * j:PIECE * j + 8, :]
    carry = jnp.zeros((8, 128), F32)
    for j in range(blocks - 1, -1, -1):
        out_ref[8 * j:8 * j + 8, :] = jnp.where(forward, held[j], carry)
        carry = carry * in_ref[PIECE * j + 8:PIECE * j + 9, :] + in_ref[PIECE * j:PIECE * j + 8, :]


def read_states(st_ref):
    both = []
    for kind in range(2):
        halves = []
        for half in range(2):
            halves.append(jnp.concatenate(
                [st_ref[pl.ds(256 * half + 4 * kind + i, 32, stride=8), :] for i in range(4)],
                axis=0))
        both.append(jnp.concatenate(halves, axis=1))
    return both


def local_part(len_ref, ld_ref, dt_ref, w_ref, r_ref, x_ref, g_ref,
               y_ref, p_ref, wl_ref, rl_ref, xh_ref, xl_ref, gh_ref, gl_ref):
    heads, steps = ld_ref.shape
    chunks = steps // CHUNK
    offset = block_start(steps)
    ld = ld_ref[...]
    dt_all = dt_ref[...]
    enter_b, leave_b, _ = block_rows(len_ref, offset, ld, dt_all)
    parts = running_sums(ld)
    low = iota((CHUNK, 128), 1) < 64
    causal = iota((CHUNK, CHUNK), 1) <= iota((CHUNK, CHUNK), 0)
    saved = []
    for q in range(chunks):
        rows = pl.ds(q * CHUNK, CHUNK)
        span = slice(q * CHUNK, (q + 1) * CHUNK)
        first = offset + q * CHUNK
        cum = parts[q]
        total = cum[:, CHUNK - 1:CHUNK]
        dt = dt_all[:, span]
        rec_row = records_at(len_ref, first + iota((1, CHUNK), 1))
        rec_col = records_at(len_ref, first + iota((CHUNK, 1), 0))
        last = scalar_record(len_ref, first + CHUNK - 1)
        prev = scalar_record(len_ref, first - 1)
        enter = jnp.exp(jnp.where(rec_row == prev, cum, NEG))
        leave = jnp.exp(jnp.where(rec_row == last, total - cum, NEG))
        keep = jnp.exp(jnp.where(last == prev, total, NEG))
        stack = jnp.concatenate(
            [cum, enter, leave, leave * dt, leave_b[:, span] * dt, enter_b[:, span]], axis=0)
        cols = jnp.transpose(stack)
        x = x_ref[rows, :]
        g = g_ref[rows, :]
        xf = x.astype(F32)
        gf = g.astype(F32)
        xb_hi, xb_lo = split(xf * lanes_of(cols, 4 * heads, heads))
        gb_hi, gb_lo = split(gf * lanes_of(cols, 5 * heads, heads))
        xh_ref[rows, :] = xb_hi
        xl_ref[rows, :] = xb_lo
        gh_ref[rows, :] = gb_hi
        gl_ref[rows, :] = gb_lo
        enter_lanes = lanes_of(cols, heads, heads)
        leave_lanes = lanes_of(cols, 2 * heads, heads)
        xc = split(xf * lanes_of(cols, 3 * heads, heads))
        gc = split(gf * enter_lanes)
        w = w_ref[rows, :]
        r = r_ref[rows, :]
        fresh = mm(w, xc[0], 0, 0) + mm(w, xc[1], 0, 0)
        back = mm(r, gc[0], 0, 0) + mm(r, gc[1], 0, 0)
        keep_row = jnp.concatenate([
            jnp.where(iota((1, 128), 1) < 64, keep[h:h + 1, :], keep[h + 1:h + 2, :])
            for h in range(0, heads, 2)], axis=1)
        inside = causal & (rec_row == rec_col)
        scores = mm(r, w, 1, 1)
        total_e = jnp.zeros((CHUNK, CHUNK), F32)
        y_parts, p_parts = [], []
        for h in range(heads):
            pair = slice(128 * (h // 2), 128 * (h // 2) + 128)
            x_pair = x[:, pair]
            g_pair = g[:, pair]
            mine = low if h % 2 == 0 else ~low
            decays = jnp.exp(jnp.where(inside, cols[:, h:h + 1] - cum[h:h + 1, :], NEG))
            weighted = scores * decays
            dt_row = dt[h:h + 1, :]
            a_hi, a_lo = split(weighted * dt_row)
            y_parts.append(mm(a_hi, x_pair, 1, 0) + mm(a_lo, x_pair, 1, 0))
            b_hi, b_lo = split(weighted)
            p_parts.append(mm(b_hi, g_pair, 0, 0) + mm(b_lo, g_pair, 0, 0))
            g_mine = jnp.where(mine, gf[:, pair], 0.0).astype(BF16)
            total_e = total_e + decays * dt_row * mm(g_mine, x_pair, 1, 1)
        y = jnp.concatenate([jnp.where(low, y_parts[h], y_parts[h + 1]) for h in range(0, heads, 2)], axis=1)
        p = jnp.concatenate([jnp.where(low, p_parts[h], p_parts[h + 1]) for h in range(0, heads, 2)], axis=1)
        e_hi, e_lo = split(total_e)
        wl = mm(e_hi, r, 0, 0) + mm(e_lo, r, 0, 0)
        rl = mm(e_hi, w, 1, 0) + mm(e_lo, w, 1, 0)
        saved.append((rows, y, p, wl, rl, xc, gc, w, r, fresh, back, keep_row, enter_lanes, leave_lanes))
    state = None
    for q in range(chunks):
        rows, y, p, wl, rl, xc, gc, w, r, fresh, back, keep_row, enter_lanes, leave_lanes = saved[q]
        if state is not None:
            s_hi, s_lo = split(state)
            y = y + enter_lanes * (mm(r, s_hi, 1, 0) + mm(r, s_lo, 1, 0))
            rl = rl + (mm(gc[0], s_hi, 1, 1) + mm(gc[0], s_lo, 1, 1) + mm(gc[1], s_hi, 1, 1))
            state = state * keep_row + fresh
        else:
            state = fresh
        y_ref[rows, :] = y
        rl_ref[rows, :] = rl
    future = None
    for q in range(chunks - 1, -1, -1):
        rows, y, p, wl, rl, xc, gc, w, r, fresh, back, keep_row, enter_lanes, leave_lanes = saved[q]
        if future is not None:
            f_hi, f_lo = split(future)
            p = p + leave_lanes * (mm(w, f_hi, 1, 0) + mm(w, f_lo, 1, 0))
            wl = wl + (mm(xc[0], f_hi, 1, 1) + mm(xc[0], f_lo, 1, 1) + mm(xc[1], f_hi, 1, 1))
            future = future * keep_row + back
        else:
            future = back
        p_ref[rows, :] = p
        wl_ref[rows, :] = wl


def shared_grads(other, st_ref, wl_ref, rl_ref, xh_ref, xl_ref, gh_ref, gl_ref, out_ref):
    groups, double, _ = out_ref.shape
    share = double // 2
    core = lax.rem(lax.axis_index("head"), 2)
    core = 1 - core if other else core
    incoming, future = read_states(st_ref)
    s_hi, s_lo = split(incoming)
    f_hi, f_lo = split(future)

    def mine(ref):
        return jnp.concatenate([
            ref[pl.ds(pl.multiple_of((2 * z + core) * share, share), share), :] for z in range(groups)], axis=0)

    xh = mine(xh_ref)
    gh = mine(gh_ref)
    w = mine(wl_ref) + mm(xh, f_hi, 1, 1) + mm(xh, f_lo, 1, 1) + mm(mine(xl_ref), f_hi, 1, 1)
    r = mine(rl_ref) + mm(gh, s_hi, 1, 1) + mm(gh, s_lo, 1, 1) + mm(mine(gl_ref), s_hi, 1, 1)
    out_ref[:, 0:share, :] = w.reshape(groups, share, w.shape[1])
    out_ref[:, share:double, :] = r.reshape(groups, share, r.shape[1])


def finish(len_ref, ld_ref, dt_ref, w_ref, r_ref, x_ref, g_ref, y_ref, p_ref, st_ref,
           out_ref, xg_ref, sg_ref, dg_ref):
    heads, steps = ld_ref.shape
    chunks = steps // CHUNK
    offset = block_start(steps)
    ld = ld_ref[...]
    dt = dt_ref[...]
    enter, leave, keep = block_rows(len_ref, offset, ld, dt)
    incoming, future = read_states(st_ref)
    s_hi, s_lo = split(incoming)
    f_hi, f_lo = split(future)
    width = x_ref.shape[1]
    pick = (iota((8, width), 1) // 64 == iota((8, width), 0)).astype(F32)
    stack = jnp.concatenate([enter, leave, dt, dt], axis=0)
    p_rows, ql_rows, qs_rows = [], [], []
    for q in range(chunks):
        rows = pl.ds(q * CHUNK, CHUNK)
        cols = jnp.transpose(stack[:, q * CHUNK:(q + 1) * CHUNK])
        r = r_ref[rows, :]
        w = w_ref[rows, :]
        y = y_ref[rows, :] + lanes_of(cols, 0, heads) * (mm(r, s_hi, 1, 0) + mm(r, s_lo, 1, 0))
        near = p_ref[rows, :]
        far = lanes_of(cols, heads, heads) * (mm(w, f_hi, 1, 0) + mm(w, f_lo, 1, 0))
        out_ref[rows, :] = y.astype(BF16)
        xg_ref[rows, :] = (lanes_of(cols, 2 * heads, heads) * (near + far)).astype(BF16)
        xf = x_ref[rows, :].astype(F32)
        p_rows.append(mm_exact(pick, g_ref[rows, :].astype(F32) * y, 1, 1)[0:heads, :])
        ql_rows.append(mm_exact(pick, xf * near, 1, 1)[0:heads, :])
        qs_rows.append(mm_exact(pick, xf * far, 1, 1)[0:heads, :])
    both = jnp.sum((incoming * future).reshape(16, 8, width), axis=0)
    cross = keep * jnp.sum(mm_exact(pick, both, 1, 1), axis=1, keepdims=True)[0:heads, :]
    ql = jnp.concatenate(ql_rows, axis=1) * dt
    qs = jnp.concatenate(qs_rows, axis=1) * dt
    pt = jnp.concatenate(p_rows, axis=1)
    sg_ref[...] = ql + qs
    diff = pt - ql
    d_in = running_sums(diff)
    q_in = running_sums(qs)
    d_tot = [d[:, CHUNK - 1:CHUNK] for d in d_in]
    later = jnp.zeros((heads, 1), F32)
    tails = [None] * chunks
    for q in range(chunks - 1, -1, -1):
        span = slice(q * CHUNK, (q + 1) * CHUNK)
        later = later + d_tot[q]
        tails[q] = later - d_in[q] + diff[:, span]
    before = cross
    for q in range(chunks):
        span = slice(q * CHUNK, (q + 1) * CHUNK)
        total = tails[q] + before + q_in[q] - qs[:, span]
        dg_ref[:, span] = ld[:, span] * total
        before = before + q_in[q][:, CHUNK - 1:CHUNK]


def add_heads(in_ref, w_ref, r_ref):
    total = jnp.sum(in_ref[...], axis=0)
    share = w_ref.shape[0]
    w_ref[...] = total[0:share, :]
    r_ref[...] = total[share:2 * share, :]


def call(kernel, outs, args, name, flops=0, moved=0, scratch=(), fetched=False, limit=40):
    smem = pl.BlockSpec(memory_space=pltpu.SMEM)
    vmem = pl.BlockSpec(memory_space=pltpu.VMEM)
    hbm = pl.BlockSpec(memory_space=pltpu.HBM)
    return pl.pallas_call(
        kernel,
        out_shape=outs,
        in_specs=[hbm if fetched else smem if a.dtype == jnp.int32 else vmem for a in args],
        out_specs=jax.tree.map(lambda _: hbm if fetched else vmem, outs),
        scratch_shapes=list(scratch),
        compiler_params=pltpu.CompilerParams(vmem_limit_bytes=limit * 1024 * 1024),
        cost_estimate=pl.CostEstimate(flops=flops, bytes_accessed=moved, transcendentals=0),
        name=name,
    )(*args)


def state_terms_call(common, blocks):
    out = jax.ShapeDtypeStruct((blocks * PIECE, 128), F32)
    buffers = [pltpu.SMEM(common[0].shape, common[0].dtype)]
    buffers += [pltpu.VMEM(a.shape, a.dtype) for a in common[1:] + (out,)]
    buffers.append(pltpu.SemaphoreType.DMA((9,)))
    return call(state_terms, out, common, "state_terms", 200_000_000, 2_000_000, buffers, True, 60)


def shards(inputs, write_map, read_map, step_scale, log_decay, lengths, out_grad):
    steps, width = inputs.shape
    heads = step_scale.shape[0]
    state = write_map.shape[1]
    blocks = lax.axis_size("ctx")
    groups = lax.axis_size("head")
    share = steps // groups
    sds = jax.ShapeDtypeStruct
    common = (lengths, log_decay, step_scale, write_map, read_map, inputs, out_grad)
    pay = state_terms_call(common, blocks)
    pay, common = lax.optimization_barrier((pay, common))
    got = lax.all_to_all(pay.reshape(blocks, 1, PIECE * 128), "ctx", 0, 0)
    y, p, wl, rl, xh, xl, gh, gl = call(
        local_part,
        [sds((steps, width), F32), sds((steps, width), F32), sds((steps, state), F32), sds((steps, state), F32)]
        + [sds((steps, width), BF16)] * 4,
        common, "local_part", 4_000_000_000, 20_000_000)
    got, wl, rl = lax.optimization_barrier((got, wl, rl))
    scanned = call(scan_blocks, sds((blocks * 8, 128), F32), (got.reshape(blocks * PIECE, 128),), "scan_blocks", 1_000_000, 1_000_000)
    states = lax.all_to_all(scanned.reshape(blocks, 8, 128), "ctx", 0, 0).reshape(blocks * 8, 128)
    parts = (states, wl, rl, xh, xl, gh, gl)
    half = sds((groups // 2, 2 * share, state), F32)
    theirs = call(functools.partial(shared_grads, True), half, parts, "shared_grads_other", 100_000_000, 1_000_000)
    ours = call(functools.partial(shared_grads, False), half, parts, "shared_grads_own", 100_000_000, 1_000_000)
    swapped = lax.ppermute(theirs, "head", [(i, i ^ 1) for i in range(groups)])
    terms, y = lax.optimization_barrier((ours + swapped, y))
    cores = [[2 * z + c for z in range(groups // 2)] for c in range(2)]
    summed = lax.all_to_all(terms, "head", 0, 0, axis_index_groups=cores)
    outputs, input_grad, step_grad, decay_grad = call(
        finish,
        [sds((steps, width), BF16), sds((steps, width), BF16), sds((heads, steps), F32), sds((heads, steps), F32)],
        common + (y, p, states), "finish", 4_000_000_000, 20_000_000)
    write_grad, read_grad = call(
        add_heads, [sds((share, state), F32), sds((share, state), F32)], (summed,), "add_heads", 1_000_000, 1_000_000)
    return (outputs, input_grad, write_grad, read_grad, step_grad, decay_grad)


def solution(mesh):
    placed = (
        P("ctx", "head"),
        P("ctx", None),
        P("ctx", None),
        P("head", "ctx"),
        P("head", "ctx"),
        P(),
        P("ctx", "head"),
    )
    return jax.shard_map(
        shards,
        mesh=mesh,
        in_specs=placed,
        out_specs=(
            P("ctx", "head"),
            P("ctx", "head"),
            P(("ctx", "head"), None),
            P(("ctx", "head"), None),
            P("head", "ctx"),
            P("head", "ctx"),
        ),
        check_vma=False,
    )
```

```python
import functools

import jax
import jax.numpy as jnp
from jax import lax
from jax.experimental import pallas as pl
from jax.experimental.pallas import tpu as pltpu
from jax.sharding import PartitionSpec as P

F32 = jnp.float32
BF16 = jnp.bfloat16
CHUNK = 128
NEG = -1e30
PIECE = 9


def split(v):
    hi = v.astype(BF16)
    return hi, (v - hi.astype(F32)).astype(BF16)


def mm(a, b, ca, cb):
    return lax.dot_general(a, b, (((ca,), (cb,)), ((), ())), preferred_element_type=F32)


def mm_exact(a, b, ca, cb):
    return lax.dot_general(
        a, b, (((ca,), (cb,)), ((), ())),
        precision=lax.Precision.HIGHEST, preferred_element_type=F32,
    )


def iota(shape, dim):
    return lax.broadcasted_iota(jnp.int32, shape, dim)


def records_at(len_ref, pos):
    start = jnp.int32(0)
    total = (pos >= start).astype(jnp.int32)
    for k in range(len_ref.shape[0] - 1):
        start = start + len_ref[k]
        total = total + (pos >= start).astype(jnp.int32)
    return total


def scalar_record(len_ref, pos):
    start = jnp.int32(0)
    total = jnp.where(pos >= start, 1, 0)
    for k in range(len_ref.shape[0] - 1):
        start = start + len_ref[k]
        total = total + jnp.where(pos >= start, 1, 0)
    return total


def running_sums(rows):
    heads, steps = rows.shape
    chunks = steps // CHUNK
    stacked = jnp.concatenate([rows[:, q * CHUNK:(q + 1) * CHUNK] for q in range(chunks)], axis=0)
    tri = (iota((CHUNK, CHUNK), 0) <= iota((CHUNK, CHUNK), 1)).astype(F32)
    sums = mm_exact(stacked, tri, 1, 0)
    return [sums[q * heads:(q + 1) * heads, :] for q in range(chunks)]


def block_rows(len_ref, offset, ld, dt):
    heads, steps = ld.shape
    parts = running_sums(ld)
    total = jnp.zeros((heads, 1), F32)
    cums = []
    for part in parts:
        cums.append(part + total)
        total = total + part[:, CHUNK - 1:CHUNK]
    cum = jnp.concatenate(cums, axis=1)
    rec = records_at(len_ref, offset + iota((1, steps), 1))
    last = scalar_record(len_ref, offset + steps - 1)
    prev = scalar_record(len_ref, offset - 1)
    enter = jnp.exp(jnp.where(rec == prev, cum, NEG))
    leave = jnp.exp(jnp.where(rec == last, total - cum, NEG))
    keep = jnp.exp(jnp.where(last == prev, total, NEG))
    return enter, leave, keep


def lanes_of(cols, first, heads):
    rows = cols.shape[0]
    low = iota((rows, 128), 1) < 64
    out = []
    for h in range(0, heads, 2):
        a = cols[:, first + h:first + h + 1]
        b = cols[:, first + h + 1:first + h + 2]
        out.append(jnp.where(low, a, b))
    return jnp.concatenate(out, axis=1)


def block_start(steps):
    return lax.axis_index("ctx") * steps


def state_terms(len_hbm, ld_hbm, dt_hbm, w_hbm, r_hbm, x_hbm, g_hbm, pay_hbm,
                len_ref, ld_ref, dt_ref, w_ref, r_ref, x_ref, g_ref, pay_ref, sems):
    pairs = ((len_hbm, len_ref), (ld_hbm, ld_ref), (dt_hbm, dt_ref), (x_hbm, x_ref),
             (w_hbm, w_ref), (g_hbm, g_ref), (r_hbm, r_ref))
    copies = [pltpu.make_async_copy(src, dst, sems.at[i]) for i, (src, dst) in enumerate(pairs)]
    for copy in copies:
        copy.start()
    for copy in copies[:3]:
        copy.wait()
    heads, steps = ld_ref.shape
    dt = dt_ref[...]
    enter, leave, keep = block_rows(len_ref, block_start(steps), ld_ref[...], dt)
    stack = jnp.concatenate([leave * dt, enter], axis=0)
    cols = [jnp.transpose(stack[:, q * CHUNK:(q + 1) * CHUNK]) for q in range(steps // CHUNK)]
    low = iota((CHUNK, 128), 1) < 64

    def scaled(ref, lanes, first):
        return split(jnp.concatenate([
            ref[pl.ds(q * CHUNK, CHUNK), lanes].astype(F32)
            * jnp.where(low, cols[q][:, first:first + 1], cols[q][:, first + 1:first + 2])
            for q in range(steps // CHUNK)], axis=0))

    for copy in copies[3:]:
        copy.wait()
    w = w_ref[...]
    r = r_ref[...]
    half_rows = pay_ref.shape[0] // 2
    sends = []
    for half in range(2):
        lanes = slice(128 * half, 128 * half + 128)
        base = half_rows * half
        both = mm(w, jnp.concatenate(scaled(x_ref, lanes, 2 * half), axis=1), 0, 0)
        fresh = both[:, 0:128] + both[:, 128:256]
        both = mm(r, jnp.concatenate(scaled(g_ref, lanes, heads + 2 * half), axis=1), 0, 0)
        back = both[:, 0:128] + both[:, 128:256]
        for i in range(4):
            rows = slice(32 * i, 32 * i + 32)
            pay_ref[pl.ds(base + i, 32, stride=PIECE), :] = fresh[rows]
            pay_ref[pl.ds(base + 4 + i, 32, stride=PIECE), :] = back[rows]
        pair = jnp.where(low[0:32], keep[2 * half:2 * half + 1, :], keep[2 * half + 1:2 * half + 2, :])
        pay_ref[pl.ds(base + 8, 32, stride=PIECE), :] = pair
        span = pl.ds(base, half_rows)
        sends.append(pltpu.make_async_copy(pay_ref.at[span], pay_hbm.at[span], sems.at[len(pairs) + half]))
        sends[-1].start()
    for send in sends:
        send.wait()


def scan_blocks(in_ref, out_ref):
    blocks = in_ref.shape[0] // PIECE
    forward = iota((8, 128), 0) < 4
    carry = jnp.zeros((8, 128), F32)
    held = []
    for j in range(blocks):
        held.append(carry)
        carry = carry * in_ref[PIECE * j + 8:PIECE * j + 9, :] + in_ref[PIECE * j:PIECE * j + 8, :]
    carry = jnp.zeros((8, 128), F32)
    for j in range(blocks - 1, -1, -1):
        out_ref[8 * j:8 * j + 8, :] = jnp.where(forward, held[j], carry)
        carry = carry * in_ref[PIECE * j + 8:PIECE * j + 9, :] + in_ref[PIECE * j:PIECE * j + 8, :]


def read_states(st_ref):
    both = []
    for kind in range(2):
        halves = []
        for half in range(2):
            halves.append(jnp.concatenate(
                [st_ref[pl.ds(256 * half + 4 * kind + i, 32, stride=8), :] for i in range(4)],
                axis=0))
        both.append(jnp.concatenate(halves, axis=1))
    return both


def local_part(len_ref, ld_ref, dt_ref, w_ref, r_ref, x_ref, g_ref,
               y_ref, p_ref, wl_ref, rl_ref, xh_ref, xl_ref, gh_ref, gl_ref):
    heads, steps = ld_ref.shape
    chunks = steps // CHUNK
    offset = block_start(steps)
    ld = ld_ref[...]
    dt_all = dt_ref[...]
    enter_b, leave_b, _ = block_rows(len_ref, offset, ld, dt_all)
    parts = running_sums(ld)
    low = iota((CHUNK, 128), 1) < 64
    causal = iota((CHUNK, CHUNK), 1) <= iota((CHUNK, CHUNK), 0)
    saved = []
    for q in range(chunks):
        rows = pl.ds(q * CHUNK, CHUNK)
        span = slice(q * CHUNK, (q + 1) * CHUNK)
        first = offset + q * CHUNK
        cum = parts[q]
        total = cum[:, CHUNK - 1:CHUNK]
        dt = dt_all[:, span]
        rec_row = records_at(len_ref, first + iota((1, CHUNK), 1))
        rec_col = records_at(len_ref, first + iota((CHUNK, 1), 0))
        last = scalar_record(len_ref, first + CHUNK - 1)
        prev = scalar_record(len_ref, first - 1)
        enter = jnp.exp(jnp.where(rec_row == prev, cum, NEG))
        leave = jnp.exp(jnp.where(rec_row == last, total - cum, NEG))
        keep = jnp.exp(jnp.where(last == prev, total, NEG))
        stack = jnp.concatenate(
            [cum, enter, leave, leave * dt, leave_b[:, span] * dt, enter_b[:, span]], axis=0)
        cols = jnp.transpose(stack)
        x = x_ref[rows, :]
        g = g_ref[rows, :]
        xf = x.astype(F32)
        gf = g.astype(F32)
        xb_hi, xb_lo = split(xf * lanes_of(cols, 4 * heads, heads))
        gb_hi, gb_lo = split(gf * lanes_of(cols, 5 * heads, heads))
        xh_ref[rows, :] = xb_hi
        xl_ref[rows, :] = xb_lo
        gh_ref[rows, :] = gb_hi
        gl_ref[rows, :] = gb_lo
        enter_lanes = lanes_of(cols, heads, heads)
        leave_lanes = lanes_of(cols, 2 * heads, heads)
        xc = split(xf * lanes_of(cols, 3 * heads, heads))
        gc = split(gf * enter_lanes)
        w = w_ref[rows, :]
        r = r_ref[rows, :]
        two = lambda m: jnp.concatenate([m, m], axis=0)
        fresh = mm(two(w), jnp.concatenate(xc, axis=0), 0, 0)
        back = mm(two(r), jnp.concatenate(gc, axis=0), 0, 0)
        keep_row = jnp.concatenate([
            jnp.where(iota((1, 128), 1) < 64, keep[h:h + 1, :], keep[h + 1:h + 2, :])
            for h in range(0, heads, 2)], axis=1)
        inside = causal & (rec_row == rec_col)
        scores = mm(r, w, 1, 1)
        total_e = jnp.zeros((CHUNK, CHUNK), F32)
        y_parts, p_parts = [], []
        for first_head in range(0, heads, 2):
            pair = slice(64 * first_head, 64 * first_head + 128)
            x_pair = x[:, pair]
            g_pair = g[:, pair]
            g_both = jnp.concatenate([
                jnp.where(low, gf[:, pair], 0.0).astype(BF16), jnp.where(low, 0.0, gf[:, pair]).astype(BF16)], axis=0)
            dots = mm(g_both, x_pair, 1, 1)
            forward, backward = [], []
            for k in range(2):
                h = first_head + k
                decays = jnp.exp(jnp.where(inside, cols[:, h:h + 1] - cum[h:h + 1, :], NEG))
                weighted = scores * decays
                dt_row = dt[h:h + 1, :]
                forward.append(jnp.concatenate(split(weighted * dt_row), axis=1))
                backward.append(jnp.concatenate(split(weighted), axis=0))
                total_e = total_e + decays * dt_row * dots[k * CHUNK:(k + 1) * CHUNK, :]
            y2 = mm(jnp.concatenate(forward, axis=0), jnp.concatenate([x_pair, x_pair], axis=0), 1, 0)
            p2 = mm(jnp.concatenate(backward, axis=1), jnp.concatenate([g_pair, g_pair], axis=0), 0, 0)
            y_parts.append(jnp.where(low, y2[0:CHUNK], y2[CHUNK:2 * CHUNK]))
            p_parts.append(jnp.where(low, p2[0:CHUNK], p2[CHUNK:2 * CHUNK]))
        y = jnp.concatenate(y_parts, axis=1)
        p = jnp.concatenate(p_parts, axis=1)
        e_hi, e_lo = split(total_e)
        wl = mm(jnp.concatenate([e_hi, e_lo], axis=0), two(r), 0, 0)
        rl = mm(jnp.concatenate([e_hi, e_lo], axis=1), two(w), 1, 0)
        saved.append((rows, y, p, wl, rl, xc, gc, w, r, fresh, back, keep_row, enter_lanes, leave_lanes))
    state = None
    for q in range(chunks):
        rows, y, p, wl, rl, xc, gc, w, r, fresh, back, keep_row, enter_lanes, leave_lanes = saved[q]
        if state is not None:
            s_hi, s_lo = split(state)
            y = y + enter_lanes * mm(jnp.concatenate([r, r], axis=1), jnp.concatenate([s_hi, s_lo], axis=0), 1, 0)
            rl = rl + (mm(gc[0], s_hi, 1, 1) + mm(gc[0], s_lo, 1, 1) + mm(gc[1], s_hi, 1, 1))
            state = state * keep_row + fresh
        else:
            state = fresh
        y_ref[rows, :] = y
        rl_ref[rows, :] = rl
    future = None
    for q in range(chunks - 1, -1, -1):
        rows, y, p, wl, rl, xc, gc, w, r, fresh, back, keep_row, enter_lanes, leave_lanes = saved[q]
        if future is not None:
            f_hi, f_lo = split(future)
            p = p + leave_lanes * mm(jnp.concatenate([w, w], axis=1), jnp.concatenate([f_hi, f_lo], axis=0), 1, 0)
            wl = wl + (mm(xc[0], f_hi, 1, 1) + mm(xc[0], f_lo, 1, 1) + mm(xc[1], f_hi, 1, 1))
            future = future * keep_row + back
        else:
            future = back
        p_ref[rows, :] = p
        wl_ref[rows, :] = wl


def shared_grads(other, st_ref, wl_ref, rl_ref, xh_ref, xl_ref, gh_ref, gl_ref, out_ref):
    groups, double, _ = out_ref.shape
    share = double // 2
    core = lax.rem(lax.axis_index("head"), 2)
    core = 1 - core if other else core
    incoming, future = read_states(st_ref)
    s_hi, s_lo = split(incoming)
    f_hi, f_lo = split(future)

    def mine(ref):
        return jnp.concatenate([
            ref[pl.ds(pl.multiple_of((2 * z + core) * share, share), share), :] for z in range(groups)], axis=0)

    xh = mine(xh_ref)
    gh = mine(gh_ref)
    w = mine(wl_ref) + mm(xh, f_hi, 1, 1) + mm(xh, f_lo, 1, 1) + mm(mine(xl_ref), f_hi, 1, 1)
    r = mine(rl_ref) + mm(gh, s_hi, 1, 1) + mm(gh, s_lo, 1, 1) + mm(mine(gl_ref), s_hi, 1, 1)
    out_ref[:, 0:share, :] = w.reshape(groups, share, w.shape[1])
    out_ref[:, share:double, :] = r.reshape(groups, share, r.shape[1])


def finish(len_ref, ld_ref, dt_ref, w_ref, r_ref, x_ref, g_ref, y_ref, p_ref, st_ref,
           out_ref, xg_ref, sg_ref, dg_ref):
    heads, steps = ld_ref.shape
    chunks = steps // CHUNK
    offset = block_start(steps)
    ld = ld_ref[...]
    dt = dt_ref[...]
    enter, leave, keep = block_rows(len_ref, offset, ld, dt)
    incoming, future = read_states(st_ref)
    s_hi, s_lo = split(incoming)
    f_hi, f_lo = split(future)
    width = x_ref.shape[1]
    pick = (iota((8, width), 1) // 64 == iota((8, width), 0)).astype(F32)
    stack = jnp.concatenate([enter, leave, dt, dt], axis=0)
    p_rows, ql_rows, qs_rows = [], [], []
    for q in range(chunks):
        rows = pl.ds(q * CHUNK, CHUNK)
        cols = jnp.transpose(stack[:, q * CHUNK:(q + 1) * CHUNK])
        r = r_ref[rows, :]
        w = w_ref[rows, :]
        y = y_ref[rows, :] + lanes_of(cols, 0, heads) * (mm(r, s_hi, 1, 0) + mm(r, s_lo, 1, 0))
        near = p_ref[rows, :]
        far = lanes_of(cols, heads, heads) * (mm(w, f_hi, 1, 0) + mm(w, f_lo, 1, 0))
        out_ref[rows, :] = y.astype(BF16)
        xg_ref[rows, :] = (lanes_of(cols, 2 * heads, heads) * (near + far)).astype(BF16)
        xf = x_ref[rows, :].astype(F32)
        p_rows.append(mm_exact(pick, g_ref[rows, :].astype(F32) * y, 1, 1)[0:heads, :])
        ql_rows.append(mm_exact(pick, xf * near, 1, 1)[0:heads, :])
        qs_rows.append(mm_exact(pick, xf * far, 1, 1)[0:heads, :])
    both = jnp.sum((incoming * future).reshape(16, 8, width), axis=0)
    cross = keep * jnp.sum(mm_exact(pick, both, 1, 1), axis=1, keepdims=True)[0:heads, :]
    ql = jnp.concatenate(ql_rows, axis=1) * dt
    qs = jnp.concatenate(qs_rows, axis=1) * dt
    pt = jnp.concatenate(p_rows, axis=1)
    sg_ref[...] = ql + qs
    diff = pt - ql
    d_in = running_sums(diff)
    q_in = running_sums(qs)
    d_tot = [d[:, CHUNK - 1:CHUNK] for d in d_in]
    later = jnp.zeros((heads, 1), F32)
    tails = [None] * chunks
    for q in range(chunks - 1, -1, -1):
        span = slice(q * CHUNK, (q + 1) * CHUNK)
        later = later + d_tot[q]
        tails[q] = later - d_in[q] + diff[:, span]
    before = cross
    for q in range(chunks):
        span = slice(q * CHUNK, (q + 1) * CHUNK)
        total = tails[q] + before + q_in[q] - qs[:, span]
        dg_ref[:, span] = ld[:, span] * total
        before = before + q_in[q][:, CHUNK - 1:CHUNK]


def add_heads(in_ref, w_ref, r_ref):
    total = jnp.sum(in_ref[...], axis=0)
    share = w_ref.shape[0]
    w_ref[...] = total[0:share, :]
    r_ref[...] = total[share:2 * share, :]


def call(kernel, outs, args, name, flops=0, moved=0, scratch=(), fetched=False, limit=40):
    smem = pl.BlockSpec(memory_space=pltpu.SMEM)
    vmem = pl.BlockSpec(memory_space=pltpu.VMEM)
    hbm = pl.BlockSpec(memory_space=pltpu.HBM)
    return pl.pallas_call(
        kernel,
        out_shape=outs,
        in_specs=[hbm if fetched else smem if a.dtype == jnp.int32 else vmem for a in args],
        out_specs=jax.tree.map(lambda _: hbm if fetched else vmem, outs),
        scratch_shapes=list(scratch),
        compiler_params=pltpu.CompilerParams(vmem_limit_bytes=limit * 1024 * 1024),
        cost_estimate=pl.CostEstimate(flops=flops, bytes_accessed=moved, transcendentals=0),
        name=name,
    )(*args)


def state_terms_call(common, blocks):
    out = jax.ShapeDtypeStruct((blocks * PIECE, 128), F32)
    buffers = [pltpu.SMEM(common[0].shape, common[0].dtype)]
    buffers += [pltpu.VMEM(a.shape, a.dtype) for a in common[1:] + (out,)]
    buffers.append(pltpu.SemaphoreType.DMA((9,)))
    return call(state_terms, out, common, "state_terms", 200_000_000, 2_000_000, buffers, True, 60)


def shards(inputs, write_map, read_map, step_scale, log_decay, lengths, out_grad):
    steps, width = inputs.shape
    heads = step_scale.shape[0]
    state = write_map.shape[1]
    blocks = lax.axis_size("ctx")
    groups = lax.axis_size("head")
    share = steps // groups
    sds = jax.ShapeDtypeStruct
    common = (lengths, log_decay, step_scale, write_map, read_map, inputs, out_grad)
    pay = state_terms_call(common, blocks)
    pay, common = lax.optimization_barrier((pay, common))
    got = lax.all_to_all(pay.reshape(blocks, 1, PIECE * 128), "ctx", 0, 0)
    y, p, wl, rl, xh, xl, gh, gl = call(
        local_part,
        [sds((steps, width), F32), sds((steps, width), F32), sds((steps, state), F32), sds((steps, state), F32)]
        + [sds((steps, width), BF16)] * 4,
        common, "local_part", 4_000_000_000, 20_000_000)
    got, wl, rl = lax.optimization_barrier((got, wl, rl))
    scanned = call(scan_blocks, sds((blocks * 8, 128), F32), (got.reshape(blocks * PIECE, 128),), "scan_blocks", 1_000_000, 1_000_000)
    states = lax.all_to_all(scanned.reshape(blocks, 8, 128), "ctx", 0, 0).reshape(blocks * 8, 128)
    parts = (states, wl, rl, xh, xl, gh, gl)
    half = sds((groups // 2, 2 * share, state), F32)
    theirs = call(functools.partial(shared_grads, True), half, parts, "shared_grads_other", 100_000_000, 1_000_000)
    ours = call(functools.partial(shared_grads, False), half, parts, "shared_grads_own", 100_000_000, 1_000_000)
    swapped = lax.ppermute(theirs, "head", [(i, i ^ 1) for i in range(groups)])
    terms, y = lax.optimization_barrier((ours + swapped, y))
    cores = [[2 * z + c for z in range(groups // 2)] for c in range(2)]
    summed = lax.all_to_all(terms, "head", 0, 0, axis_index_groups=cores)
    outputs, input_grad, step_grad, decay_grad = call(
        finish,
        [sds((steps, width), BF16), sds((steps, width), BF16), sds((heads, steps), F32), sds((heads, steps), F32)],
        common + (y, p, states), "finish", 4_000_000_000, 20_000_000)
    write_grad, read_grad = call(
        add_heads, [sds((share, state), F32), sds((share, state), F32)], (summed,), "add_heads", 1_000_000, 1_000_000)
    return (outputs, input_grad, write_grad, read_grad, step_grad, decay_grad)


def solution(mesh):
    placed = (
        P("ctx", "head"),
        P("ctx", None),
        P("ctx", None),
        P("head", "ctx"),
        P("head", "ctx"),
        P(),
        P("ctx", "head"),
    )
    return jax.shard_map(
        shards,
        mesh=mesh,
        in_specs=placed,
        out_specs=(
            P("ctx", "head"),
            P("ctx", "head"),
            P(("ctx", "head"), None),
            P(("ctx", "head"), None),
            P("head", "ctx"),
            P("head", "ctx"),
        ),
        check_vma=False,
    )
```

```python
import functools

import jax
import jax.numpy as jnp
from jax import lax
from jax.experimental import pallas as pl
from jax.experimental.pallas import tpu as pltpu
from jax.sharding import PartitionSpec as P

F32 = jnp.float32
BF16 = jnp.bfloat16
CHUNK = 128
NEG = -1e30
PIECE = 9


def split(v):
    hi = v.astype(BF16)
    return hi, (v - hi.astype(F32)).astype(BF16)


def mm(a, b, ca, cb):
    return lax.dot_general(a, b, (((ca,), (cb,)), ((), ())), preferred_element_type=F32)


def mm_exact(a, b, ca, cb):
    return lax.dot_general(
        a, b, (((ca,), (cb,)), ((), ())),
        precision=lax.Precision.HIGHEST, preferred_element_type=F32,
    )


def iota(shape, dim):
    return lax.broadcasted_iota(jnp.int32, shape, dim)


def records_at(len_ref, pos):
    start = jnp.int32(0)
    total = (pos >= start).astype(jnp.int32)
    for k in range(len_ref.shape[0] - 1):
        start = start + len_ref[k]
        total = total + (pos >= start).astype(jnp.int32)
    return total


def scalar_record(len_ref, pos):
    start = jnp.int32(0)
    total = jnp.where(pos >= start, 1, 0)
    for k in range(len_ref.shape[0] - 1):
        start = start + len_ref[k]
        total = total + jnp.where(pos >= start, 1, 0)
    return total


def running_sums(rows):
    heads, steps = rows.shape
    chunks = steps // CHUNK
    stacked = jnp.concatenate([rows[:, q * CHUNK:(q + 1) * CHUNK] for q in range(chunks)], axis=0)
    tri = (iota((CHUNK, CHUNK), 0) <= iota((CHUNK, CHUNK), 1)).astype(F32)
    sums = mm_exact(stacked, tri, 1, 0)
    return [sums[q * heads:(q + 1) * heads, :] for q in range(chunks)]


def block_rows(len_ref, offset, ld, dt):
    heads, steps = ld.shape
    parts = running_sums(ld)
    total = jnp.zeros((heads, 1), F32)
    cums = []
    for part in parts:
        cums.append(part + total)
        total = total + part[:, CHUNK - 1:CHUNK]
    cum = jnp.concatenate(cums, axis=1)
    rec = records_at(len_ref, offset + iota((1, steps), 1))
    last = scalar_record(len_ref, offset + steps - 1)
    prev = scalar_record(len_ref, offset - 1)
    enter = jnp.exp(jnp.where(rec == prev, cum, NEG))
    leave = jnp.exp(jnp.where(rec == last, total - cum, NEG))
    keep = jnp.exp(jnp.where(last == prev, total, NEG))
    return enter, leave, keep


def lanes_of(cols, first, heads):
    rows = cols.shape[0]
    low = iota((rows, 128), 1) < 64
    out = []
    for h in range(0, heads, 2):
        a = cols[:, first + h:first + h + 1]
        b = cols[:, first + h + 1:first + h + 2]
        out.append(jnp.where(low, a, b))
    return jnp.concatenate(out, axis=1)


def block_start(steps):
    return lax.axis_index("ctx") * steps


def state_terms(len_hbm, ld_hbm, dt_hbm, w_hbm, r_hbm, x_hbm, g_hbm, pay_hbm,
                len_ref, ld_ref, dt_ref, w_ref, r_ref, x_ref, g_ref, pay_ref, sems):
    pairs = ((len_hbm, len_ref), (ld_hbm, ld_ref), (dt_hbm, dt_ref), (x_hbm, x_ref),
             (w_hbm, w_ref), (g_hbm, g_ref), (r_hbm, r_ref))
    copies = [pltpu.make_async_copy(src, dst, sems.at[i]) for i, (src, dst) in enumerate(pairs)]
    for copy in copies:
        copy.start()
    for copy in copies[:3]:
        copy.wait()
    heads, steps = ld_ref.shape
    dt = dt_ref[...]
    enter, leave, keep = block_rows(len_ref, block_start(steps), ld_ref[...], dt)
    stack = jnp.concatenate([leave * dt, enter], axis=0)
    cols = [jnp.transpose(stack[:, q * CHUNK:(q + 1) * CHUNK]) for q in range(steps // CHUNK)]
    low = iota((CHUNK, 128), 1) < 64

    def scaled(ref, lanes, first):
        return split(jnp.concatenate([
            ref[pl.ds(q * CHUNK, CHUNK), lanes].astype(F32)
            * jnp.where(low, cols[q][:, first:first + 1], cols[q][:, first + 1:first + 2])
            for q in range(steps // CHUNK)], axis=0))

    for copy in copies[3:]:
        copy.wait()
    w = w_ref[...]
    r = r_ref[...]
    half_rows = pay_ref.shape[0] // 2
    sends = []
    for half in range(2):
        lanes = slice(128 * half, 128 * half + 128)
        base = half_rows * half
        both = mm(w, jnp.concatenate(scaled(x_ref, lanes, 2 * half), axis=1), 0, 0)
        fresh = both[:, 0:128] + both[:, 128:256]
        both = mm(r, jnp.concatenate(scaled(g_ref, lanes, heads + 2 * half), axis=1), 0, 0)
        back = both[:, 0:128] + both[:, 128:256]
        for i in range(4):
            rows = slice(32 * i, 32 * i + 32)
            pay_ref[pl.ds(base + i, 32, stride=PIECE), :] = fresh[rows]
            pay_ref[pl.ds(base + 4 + i, 32, stride=PIECE), :] = back[rows]
        pair = jnp.where(low[0:32], keep[2 * half:2 * half + 1, :], keep[2 * half + 1:2 * half + 2, :])
        pay_ref[pl.ds(base + 8, 32, stride=PIECE), :] = pair
        span = pl.ds(base, half_rows)
        sends.append(pltpu.make_async_copy(pay_ref.at[span], pay_hbm.at[span], sems.at[len(pairs) + half]))
        sends[-1].start()
    for send in sends:
        send.wait()


def scan_blocks(in_ref, out_ref):
    blocks = in_ref.shape[0] // PIECE
    forward = iota((8, 128), 0) < 4
    carry = jnp.zeros((8, 128), F32)
    held = []
    for j in range(blocks):
        held.append(carry)
        carry = carry * in_ref[PIECE * j + 8:PIECE * j + 9, :] + in_ref[PIECE * j:PIECE * j + 8, :]
    carry = jnp.zeros((8, 128), F32)
    for j in range(blocks - 1, -1, -1):
        out_ref[8 * j:8 * j + 8, :] = jnp.where(forward, held[j], carry)
        carry = carry * in_ref[PIECE * j + 8:PIECE * j + 9, :] + in_ref[PIECE * j:PIECE * j + 8, :]


def read_states(st_ref):
    both = []
    for kind in range(2):
        halves = []
        for half in range(2):
            halves.append(jnp.concatenate(
                [st_ref[pl.ds(256 * half + 4 * kind + i, 32, stride=8), :] for i in range(4)],
                axis=0))
        both.append(jnp.concatenate(halves, axis=1))
    return both


def local_part(len_ref, ld_ref, dt_ref, w_ref, r_ref, x_ref, g_ref,
               y_ref, p_ref, wl_ref, rl_ref, xh_ref, xl_ref, gh_ref, gl_ref):
    heads, steps = ld_ref.shape
    chunks = steps // CHUNK
    offset = block_start(steps)
    ld = ld_ref[...]
    dt_all = dt_ref[...]
    enter_b, leave_b, _ = block_rows(len_ref, offset, ld, dt_all)
    parts = running_sums(ld)
    low = iota((CHUNK, 128), 1) < 64
    causal = iota((CHUNK, CHUNK), 1) <= iota((CHUNK, CHUNK), 0)
    saved = []
    for q in range(chunks):
        rows = pl.ds(q * CHUNK, CHUNK)
        span = slice(q * CHUNK, (q + 1) * CHUNK)
        first = offset + q * CHUNK
        cum = parts[q]
        total = cum[:, CHUNK - 1:CHUNK]
        dt = dt_all[:, span]
        rec_row = records_at(len_ref, first + iota((1, CHUNK), 1))
        rec_col = records_at(len_ref, first + iota((CHUNK, 1), 0))
        last = scalar_record(len_ref, first + CHUNK - 1)
        prev = scalar_record(len_ref, first - 1)
        enter = jnp.exp(jnp.where(rec_row == prev, cum, NEG))
        leave = jnp.exp(jnp.where(rec_row == last, total - cum, NEG))
        keep = jnp.exp(jnp.where(last == prev, total, NEG))
        stack = jnp.concatenate(
            [cum, enter, leave, leave * dt, leave_b[:, span] * dt, enter_b[:, span]], axis=0)
        cols = jnp.transpose(stack)
        x = x_ref[rows, :]
        g = g_ref[rows, :]
        xf = x.astype(F32)
        gf = g.astype(F32)
        xb_hi, xb_lo = split(xf * lanes_of(cols, 4 * heads, heads))
        gb_hi, gb_lo = split(gf * lanes_of(cols, 5 * heads, heads))
        xh_ref[rows, :] = xb_hi
        xl_ref[rows, :] = xb_lo
        gh_ref[rows, :] = gb_hi
        gl_ref[rows, :] = gb_lo
        enter_lanes = lanes_of(cols, heads, heads)
        leave_lanes = lanes_of(cols, 2 * heads, heads)
        xc = split(xf * lanes_of(cols, 3 * heads, heads))
        gc = split(gf * enter_lanes)
        w = w_ref[rows, :]
        r = r_ref[rows, :]
        two = lambda m: jnp.concatenate([m, m], axis=0)
        fresh = mm(two(w), jnp.concatenate(xc, axis=0), 0, 0)
        back = mm(two(r), jnp.concatenate(gc, axis=0), 0, 0)
        keep_row = jnp.concatenate([
            jnp.where(iota((1, 128), 1) < 64, keep[h:h + 1, :], keep[h + 1:h + 2, :])
            for h in range(0, heads, 2)], axis=1)
        inside = causal & (rec_row == rec_col)
        scores = mm(r, w, 1, 1)
        total_e = jnp.zeros((CHUNK, CHUNK), F32)
        y_parts, p_parts = [], []
        for first_head in range(0, heads, 2):
            pair = slice(64 * first_head, 64 * first_head + 128)
            x_pair = x[:, pair]
            g_pair = g[:, pair]
            g_both = jnp.concatenate([
                jnp.where(low, gf[:, pair], 0.0).astype(BF16), jnp.where(low, 0.0, gf[:, pair]).astype(BF16)], axis=0)
            dots = mm(g_both, x_pair, 1, 1)
            forward, backward = [], []
            for k in range(2):
                h = first_head + k
                decays = jnp.exp(jnp.where(inside, cols[:, h:h + 1] - cum[h:h + 1, :], NEG))
                weighted = scores * decays
                dt_row = dt[h:h + 1, :]
                forward.append(jnp.concatenate(split(weighted * dt_row), axis=1))
                backward.append(jnp.concatenate(split(weighted), axis=0))
                total_e = total_e + decays * dt_row * dots[k * CHUNK:(k + 1) * CHUNK, :]
            y2 = mm(jnp.concatenate(forward, axis=0), jnp.concatenate([x_pair, x_pair], axis=0), 1, 0)
            p2 = mm(jnp.concatenate(backward, axis=1), jnp.concatenate([g_pair, g_pair], axis=0), 0, 0)
            y_parts.append(jnp.where(low, y2[0:CHUNK], y2[CHUNK:2 * CHUNK]))
            p_parts.append(jnp.where(low, p2[0:CHUNK], p2[CHUNK:2 * CHUNK]))
        y = jnp.concatenate(y_parts, axis=1)
        p = jnp.concatenate(p_parts, axis=1)
        e_hi, e_lo = split(total_e)
        wl = mm(jnp.concatenate([e_hi, e_lo], axis=0), two(r), 0, 0)
        rl = mm(jnp.concatenate([e_hi, e_lo], axis=1), two(w), 1, 0)
        saved.append((rows, y, p, wl, rl, xc, gc, w, r, fresh, back, keep_row, enter_lanes, leave_lanes))
    state = None
    for q in range(chunks):
        rows, y, p, wl, rl, xc, gc, w, r, fresh, back, keep_row, enter_lanes, leave_lanes = saved[q]
        if state is not None:
            s_hi, s_lo = split(state)
            y = y + enter_lanes * mm(jnp.concatenate([r, r], axis=1), jnp.concatenate([s_hi, s_lo], axis=0), 1, 0)
            rl = rl + (mm(gc[0], s_hi, 1, 1) + mm(gc[0], s_lo, 1, 1) + mm(gc[1], s_hi, 1, 1))
            state = state * keep_row + fresh
        else:
            state = fresh
        y_ref[rows, :] = y
        rl_ref[rows, :] = rl
    future = None
    for q in range(chunks - 1, -1, -1):
        rows, y, p, wl, rl, xc, gc, w, r, fresh, back, keep_row, enter_lanes, leave_lanes = saved[q]
        if future is not None:
            f_hi, f_lo = split(future)
            p = p + leave_lanes * mm(jnp.concatenate([w, w], axis=1), jnp.concatenate([f_hi, f_lo], axis=0), 1, 0)
            wl = wl + (mm(xc[0], f_hi, 1, 1) + mm(xc[0], f_lo, 1, 1) + mm(xc[1], f_hi, 1, 1))
            future = future * keep_row + back
        else:
            future = back
        p_ref[rows, :] = p
        wl_ref[rows, :] = wl


def shared_grads(other, st_ref, wl_ref, rl_ref, xh_ref, xl_ref, gh_ref, gl_ref, out_ref):
    groups, double, _ = out_ref.shape
    share = double // 2
    core = lax.rem(lax.axis_index("head"), 2)
    core = 1 - core if other else core
    incoming, future = read_states(st_ref)
    s_hi, s_lo = split(incoming)
    f_hi, f_lo = split(future)

    def mine(ref):
        return jnp.concatenate([
            ref[pl.ds(pl.multiple_of((2 * z + core) * share, share), share), :] for z in range(groups)], axis=0)

    xh = mine(xh_ref)
    gh = mine(gh_ref)
    w = mine(wl_ref) + mm(xh, f_hi, 1, 1) + mm(xh, f_lo, 1, 1) + mm(mine(xl_ref), f_hi, 1, 1)
    r = mine(rl_ref) + mm(gh, s_hi, 1, 1) + mm(gh, s_lo, 1, 1) + mm(mine(gl_ref), s_hi, 1, 1)
    out_ref[:, 0:share, :] = w.reshape(groups, share, w.shape[1])
    out_ref[:, share:double, :] = r.reshape(groups, share, r.shape[1])


def finish(len_ref, ld_ref, dt_ref, w_ref, r_ref, x_ref, g_ref, y_ref, p_ref, st_ref,
           out_ref, xg_ref, sg_ref, dg_ref):
    heads, steps = ld_ref.shape
    chunks = steps // CHUNK
    offset = block_start(steps)
    ld = ld_ref[...]
    dt = dt_ref[...]
    enter, leave, keep = block_rows(len_ref, offset, ld, dt)
    incoming, future = read_states(st_ref)
    s_hi, s_lo = split(incoming)
    f_hi, f_lo = split(future)
    width = x_ref.shape[1]
    pick = (iota((8, width), 1) // 64 == iota((8, width), 0)).astype(F32)
    stack = jnp.concatenate([enter, leave, dt, dt], axis=0)
    p_rows, ql_rows, qs_rows = [], [], []
    for q in range(chunks):
        rows = pl.ds(q * CHUNK, CHUNK)
        cols = jnp.transpose(stack[:, q * CHUNK:(q + 1) * CHUNK])
        r = r_ref[rows, :]
        w = w_ref[rows, :]
        y = y_ref[rows, :] + lanes_of(cols, 0, heads) * (mm(r, s_hi, 1, 0) + mm(r, s_lo, 1, 0))
        near = p_ref[rows, :]
        far = lanes_of(cols, heads, heads) * (mm(w, f_hi, 1, 0) + mm(w, f_lo, 1, 0))
        out_ref[rows, :] = y.astype(BF16)
        xg_ref[rows, :] = (lanes_of(cols, 2 * heads, heads) * (near + far)).astype(BF16)
        xf = x_ref[rows, :].astype(F32)
        p_rows.append(mm_exact(pick, g_ref[rows, :].astype(F32) * y, 1, 1)[0:heads, :])
        ql_rows.append(mm_exact(pick, xf * near, 1, 1)[0:heads, :])
        qs_rows.append(mm_exact(pick, xf * far, 1, 1)[0:heads, :])
    both = jnp.sum((incoming * future).reshape(16, 8, width), axis=0)
    cross = keep * jnp.sum(mm_exact(pick, both, 1, 1), axis=1, keepdims=True)[0:heads, :]
    ql = jnp.concatenate(ql_rows, axis=1) * dt
    qs = jnp.concatenate(qs_rows, axis=1) * dt
    pt = jnp.concatenate(p_rows, axis=1)
    sg_ref[...] = ql + qs
    diff = pt - ql
    d_in = running_sums(diff)
    q_in = running_sums(qs)
    d_tot = [d[:, CHUNK - 1:CHUNK] for d in d_in]
    later = jnp.zeros((heads, 1), F32)
    tails = [None] * chunks
    for q in range(chunks - 1, -1, -1):
        span = slice(q * CHUNK, (q + 1) * CHUNK)
        later = later + d_tot[q]
        tails[q] = later - d_in[q] + diff[:, span]
    before = cross
    for q in range(chunks):
        span = slice(q * CHUNK, (q + 1) * CHUNK)
        total = tails[q] + before + q_in[q] - qs[:, span]
        dg_ref[:, span] = ld[:, span] * total
        before = before + q_in[q][:, CHUNK - 1:CHUNK]


def add_heads(in_ref, w_ref, r_ref):
    total = jnp.sum(in_ref[...], axis=0)
    share = w_ref.shape[0]
    w_ref[...] = total[0:share, :]
    r_ref[...] = total[share:2 * share, :]


def call(kernel, outs, args, name, flops=0, moved=0, scratch=(), fetched=False, limit=40):
    smem = pl.BlockSpec(memory_space=pltpu.SMEM)
    vmem = pl.BlockSpec(memory_space=pltpu.VMEM)
    hbm = pl.BlockSpec(memory_space=pltpu.HBM)
    return pl.pallas_call(
        kernel,
        out_shape=outs,
        in_specs=[hbm if fetched else smem if a.dtype == jnp.int32 else vmem for a in args],
        out_specs=jax.tree.map(lambda _: hbm if fetched else vmem, outs),
        scratch_shapes=list(scratch),
        compiler_params=pltpu.CompilerParams(vmem_limit_bytes=limit * 1024 * 1024),
        cost_estimate=pl.CostEstimate(flops=flops, bytes_accessed=moved, transcendentals=0),
        name=name,
    )(*args)


def state_terms_call(common, blocks):
    out = jax.ShapeDtypeStruct((blocks * PIECE, 128), F32)
    buffers = [pltpu.SMEM(common[0].shape, common[0].dtype)]
    buffers += [pltpu.VMEM(a.shape, a.dtype) for a in common[1:] + (out,)]
    buffers.append(pltpu.SemaphoreType.DMA((9,)))
    return call(state_terms, out, common, "state_terms", 200_000_000, 2_000_000, buffers, True, 60)


def shards(inputs, write_map, read_map, step_scale, log_decay, lengths, out_grad):
    steps, width = inputs.shape
    heads = step_scale.shape[0]
    state = write_map.shape[1]
    blocks = lax.axis_size("ctx")
    groups = lax.axis_size("head")
    share = steps // groups
    sds = jax.ShapeDtypeStruct
    common = (lengths, log_decay, step_scale, write_map, read_map, inputs, out_grad)
    pay = state_terms_call(common, blocks)
    pay, common = lax.optimization_barrier((pay, common))
    got = lax.all_to_all(pay.reshape(blocks, 1, PIECE * 128), "ctx", 0, 0)
    y, p, wl, rl, xh, xl, gh, gl = call(
        local_part,
        [sds((steps, width), F32), sds((steps, width), F32), sds((steps, state), F32), sds((steps, state), F32)]
        + [sds((steps, width), BF16)] * 4,
        common, "local_part", 4_000_000_000, 20_000_000)
    got, wl, rl = lax.optimization_barrier((got, wl, rl))
    scanned = call(scan_blocks, sds((blocks * 8, 128), F32), (got.reshape(blocks * PIECE, 128),), "scan_blocks", 1_000_000, 1_000_000)
    states = lax.all_to_all(scanned.reshape(blocks, 8, 128), "ctx", 0, 0).reshape(blocks * 8, 128)
    parts = (states, wl, rl, xh, xl, gh, gl)
    half = sds((groups // 2, 2 * share, state), F32)
    theirs = call(functools.partial(shared_grads, True), half, parts, "shared_grads_other", 100_000_000, 1_000_000)
    ours = call(functools.partial(shared_grads, False), half, parts, "shared_grads_own", 100_000_000, 1_000_000)
    swapped = lax.ppermute(theirs, "head", [(i, i ^ 1) for i in range(groups)])
    terms, y = lax.optimization_barrier((ours + swapped, y))
    cores = [[2 * z + c for z in range(groups // 2)] for c in range(2)]
    summed = lax.all_to_all(terms, "head", 0, 0, axis_index_groups=cores)
    outputs, input_grad, step_grad, decay_grad = call(
        finish,
        [sds((steps, width), BF16), sds((steps, width), BF16), sds((heads, steps), F32), sds((heads, steps), F32)],
        common + (y, p, states), "finish", 4_000_000_000, 20_000_000)
    total = jnp.sum(summed, axis=0)
    write_grad, read_grad = total[0:share], total[share:2 * share]
    return (outputs, input_grad, write_grad, read_grad, step_grad, decay_grad)


def solution(mesh):
    placed = (
        P("ctx", "head"),
        P("ctx", None),
        P("ctx", None),
        P("head", "ctx"),
        P("head", "ctx"),
        P(),
        P("ctx", "head"),
    )
    return jax.shard_map(
        shards,
        mesh=mesh,
        in_specs=placed,
        out_specs=(
            P("ctx", "head"),
            P("ctx", "head"),
            P(("ctx", "head"), None),
            P(("ctx", "head"), None),
            P("head", "ctx"),
            P("head", "ctx"),
        ),
        check_vma=False,
    )
```
